128 devices in a mesh: dp: 32 (over x, y, core), tensor: 4 (over z).
Axes of the slice: x: 4, y: 4, z: 4, core: 2. Of those that a mesh axis runs over, the one named last changes fastest.
Arguments:
- grads_local: bfloat16 [32, 2, 8192, 1024], P('dp', None, None, 'tensor'), may hold values from -6 to 6
- params: float32 [2, 8192, 1024], P(None, 'dp', 'tensor'), may hold values from -6 to 6
- moments: float32 [3, 2, 8192, 1024], P(None, None, 'dp', 'tensor'), may hold values from -6 to 6
- row_stat: float32 [2, 8192], P(None, 'dp'), may hold values from 0.1 to 10
- col_stat: float32 [2, 1024], P(None, 'tensor'), may hold values from 0.1 to 10
- lstm_hidden: float32 [2, 512], replicated, may hold values from -0.9 to 0.9
- lstm_cell: float32 [2, 512], replicated, may hold values from -4 to 4
- lstm_input_w: float32 [5, 2048], replicated, may hold values from -2.5 to 2.5
- lstm_recur_w: float32 [512, 2048], replicated, may hold values from -0.25 to 0.25
- lstm_bias: float32 [2048], replicated, may hold values from -3 to 3
- head_w: float32 [512, 34], replicated, may hold values from -0.25 to 0.25
- head_bias: float32 [34], replicated, may hold values from -2.5 to 2.5
- mlp_first: float32 [6, 32], replicated, may hold values from -2.5 to 2.5
- mlp_second: float32 [32, 2], replicated, may hold values from -1 to 1
Outputs:
- new_params: float32 [2, 8192, 1024], P(None, 'dp', 'tensor')
- new_moments: float32 [3, 2, 8192, 1024], P(None, None, 'dp', 'tensor')
- new_rows: float32 [2, 8192], P(None, 'dp')
- new_cols: float32 [2, 1024], P(None, 'tensor')
- new_hidden: float32 [2, 512], replicated
- new_cell: float32 [2, 512], replicated
The draws below stay inside these ranges and needn't reach their ends.
All inputs are finite; a program needn't handle non-finite values.
Results may differ from the reference program's by a relative error of at most 0.0003.
Values sent between devices are 32-bit elements; how exact they have to be, the bound alone decides.
A program may use at most 128 MiB of HBM per device.

```python
import math
import jax
import jax.numpy as jnp
from jax import lax

D = 8192
KV = 1024
L = 2
H = 512
HID = 32
NF = 6
NS = 5
N_DP = 32


def with_spikes(values, rng, source, target, parts, factor):
    def block_of(position):
        return (jnp.arange(values.shape[position]) // (values.shape[position] // parts)).reshape((-1,) + (1,) * (values.ndim - 1 - position))

    first = jax.random.permutation(rng, parts)[block_of(target)]
    second = (block_of(target) + parts // 2) % parts
    return jnp.where((block_of(source) == first) | (block_of(source) == second), factor * values, values)


def level_of(key, extent, split, smallest, top_value):
    level, own = 1.0, jax.random.fold_in(key, 6)
    for position, parts in split:
        steps = jnp.exp(jax.random.uniform(jax.random.fold_in(own, position), (parts,), jnp.float32, smallest / len(split), top_value / len(split)))
        level = level * jnp.repeat(steps, extent[position] // parts).reshape([-1 if axis == position else 1 for axis in range(len(extent))])
    return level


def centred(rng, extent, scale, most, cuts=(), held_as=jnp.bfloat16):
    values = scale * jax.random.normal(rng, extent, jnp.float32)
    if cuts:
        values = values * level_of(rng, extent, cuts, -0.22, 0.18)
    return jnp.clip(values, -most, most).astype(held_as)


def noise_with(rng, dims, scale, limit, pieces, heavy, dtype=jnp.bfloat16):
    entries = scale * jax.random.normal(rng, dims, jnp.float32)
    if pieces:
        entries = entries * level_of(rng, dims, pieces, -0.22, 0.18)
    return jnp.clip(with_spikes(entries, jax.random.fold_in(rng, 3), *heavy), -limit, limit).astype(dtype)


def setup_inputs(seed: int = 0) -> dict:
    seeds = jax.random.split(jax.random.key(seed), 15)
    return {
        "grads_local": noise_with(seeds[0], (N_DP, L, D, KV), 0.2, 6.0, ((0, 32), (3, 4)), (0, 2, 32, 2.75)),
        "params": centred(seeds[1], (L, D, KV), 1.0, 6.0, ((1, 32), (2, 4)), jnp.float32),
        "moments": centred(seeds[2], (3, L, D, KV), 0.5, 6.0, ((2, 32), (3, 4)), jnp.float32),
        "row_stat": jnp.clip(jnp.exp(math.log(10.0) - 4.6051702 * jax.random.uniform(seeds[3], (L, D), jnp.float32) ** level_of(seeds[3], (L, D), ((1, 32),), -0.2, 0.2)), 0.1, 10.0),
        "col_stat": jnp.clip(jnp.exp(math.log(10.0) - 4.6051702 * jax.random.uniform(seeds[4], (L, KV), jnp.float32) ** level_of(seeds[4], (L, KV), ((1, 4),), -0.2, 0.2)), 0.1, 10.0),
        "lstm_hidden": jnp.clip(jax.random.uniform(seeds[5], (L, H), jnp.float32, -0.9, 0.9), -0.9, 0.9),
        "lstm_cell": centred(seeds[6], (L, H), 1.0, 4.0, (), jnp.float32),
        "lstm_input_w": centred(seeds[7], (NS, 4 * H), NS ** -0.5, 2.5, (), jnp.float32),
        "lstm_recur_w": centred(seeds[8], (H, 4 * H), H ** -0.5, 0.25, (), jnp.float32),
        "lstm_bias": centred(seeds[9], (4 * H,), 0.5, 3.0, (), jnp.float32),
        "head_w": centred(seeds[10], (H, HID + 2), H ** -0.5, 0.25, (), jnp.float32),
        "head_bias": centred(seeds[11], (HID + 2,), 0.6, 2.5, (), jnp.float32),
        "mlp_first": centred(seeds[12], (NF, HID), NF ** -0.5, 2.5, (), jnp.float32),
        "mlp_second": centred(seeds[13], (HID, 2), HID ** -0.5, 1.0, (), jnp.float32),
    }


HIGH = lax.Precision.HIGHEST

def lstm_step(features, hidden, cell, input_w, recur_w, bias):
    gates = jnp.dot(features, input_w, precision=HIGH) + jnp.dot(hidden, recur_w, precision=HIGH) + bias
    width = hidden.shape[1]
    in_gate = jax.nn.sigmoid(gates[:, :width])
    forget = jax.nn.sigmoid(gates[:, width:2 * width])
    candidate = jnp.tanh(gates[:, 2 * width:3 * width])
    out_gate = jax.nn.sigmoid(gates[:, 3 * width:])
    cell_next = forget * cell + in_gate * candidate
    return (out_gate * jnp.tanh(cell_next), cell_next)

def reference(grads_local, params, moments, row_stat, col_stat, lstm_hidden, lstm_cell, lstm_input_w, lstm_recur_w, lstm_bias, head_w, head_bias, mlp_first, mlp_second):

    def accumulate(total, piece):
        return (total + piece.astype(jnp.float32), None)
    grad, unused = lax.scan(accumulate, jnp.zeros(grads_local.shape[1:], jnp.float32), grads_local)
    decays = jnp.array([0.5, 0.9, 0.99], jnp.float32)[:, None, None, None]
    moments_new = decays * moments + (1.0 - decays) * grad[None]
    squares = grad * grad
    rows_new = 0.9 * row_stat + 0.1 * lax.optimization_barrier(jnp.sum(squares, 2)) / KV
    cols_new = 0.9 * col_stat + 0.1 * lax.optimization_barrier(jnp.sum(squares, 1)) / D
    row_mean = lax.optimization_barrier(jnp.sum(rows_new, 1)) / D
    count = D * KV
    means = jnp.concatenate([lax.optimization_barrier(jnp.sum(squares, (1, 2)))[:, None], lax.optimization_barrier(jnp.sum(moments_new * moments_new, (2, 3))).T, lax.optimization_barrier(jnp.sum(params * params, (1, 2)))[:, None]], 1) / count
    features = jnp.log(means + 1e-06)
    hidden_new, cell_new = lstm_step(features, lstm_hidden, lstm_cell, lstm_input_w, lstm_recur_w, lstm_bias)
    modulation = jnp.dot(hidden_new, head_w, precision=HIGH) + head_bias
    net_bias = modulation[:, :HID]
    lr_log = modulation[:, HID]
    mag_scale = modulation[:, HID + 1]
    scale = lax.rsqrt(rows_new[:, :, None] * cols_new[:, None, :] / row_mean[:, None, None] + 1e-08)
    param_norm = lax.rsqrt(means[:, 4] + 1e-06)[:, None, None]
    grad_norm = lax.rsqrt(means[:, 0] + 1e-06)[:, None, None]
    inputs = jnp.stack([grad * scale, moments_new[0] * scale, moments_new[1] * scale, moments_new[2] * scale, params * param_norm, grad * grad_norm], 1)
    blocks = 8
    inputs = inputs.reshape(L, NF, blocks, D // blocks, KV).transpose(0, 2, 1, 3, 4).reshape(L * blocks, NF, D // blocks, KV)
    biases = jnp.repeat(net_bias, blocks, axis=0)

    def network(pair):
        block_in, block_bias = pair
        hidden_units = jnp.einsum('nh,nrc->hrc', mlp_first, block_in, precision=HIGH) + block_bias[:, None, None]
        hidden_units = jnp.maximum(hidden_units, 0.0)
        return jnp.einsum('ho,hrc->orc', mlp_second, hidden_units, precision=HIGH)
    outputs = lax.map(network, (inputs, biases))
    outputs = outputs.reshape(L, blocks, 2, D // blocks, KV).transpose(0, 2, 1, 3, 4).reshape(L, 2, D, KV)
    direction = outputs[:, 0]
    magnitude = outputs[:, 1]
    step = jnp.exp(lr_log)[:, None, None] * direction * jnp.exp(0.5 * mag_scale[:, None, None] * magnitude)
    return (params - step, moments_new, rows_new, cols_new, hidden_new, cell_new)
```

```python
import functools

import jax
import jax.numpy as jnp
import numpy as np
from jax import lax
from jax.experimental import pallas as pl
from jax.experimental.pallas import tpu as pltpu
from jax.sharding import PartitionSpec as P

D = 8192
KV = 1024
L = 2
H = 512
HID = 32
NF = 6
CH = 4
NC = L * CH
RB = 256
CB = 256
RQ = RB // CH // 4
MESH = pl.DeviceIdType.MESH
F32 = jnp.float32
BF16 = jnp.bfloat16
DECAYS = tuple(np.float32(v) for v in (0.5, 0.9, 0.99))


def lane_to_rows(row):
    return jnp.transpose(jnp.broadcast_to(row, (128, 128)))


def rows_to_lane(block):
    return jnp.transpose(block)[0:1, :]


def kernel(
    grads, params, moments, row_stat, col_stat, hidden, cell, input_w, recur_w, gate_bias, head_w, head_bias, w1, w2,
    o_params, o_moms, o_rows, o_cols, o_hid, o_cell,
    graw, stage, acc, r1a, r1b, r2a, r2b,
    v_params, v_moms, v_row, v_col, v_hid, v_cell, v_iw, v_rw, v_gb, v_hw, v_hb, v_w1, v_w2,
    n_params, n_moms, n_rows, n_cols, n_hid, n_cell,
    gsum, rowrep, colacc, macc, pacc, pre, headt, hbcol, wst, w2rep, zs, zr, ps, pr, mod, norms, colrow,
    in_sem, g_sem, out_sem, s_sem, d_rs, r1a_rs, r1b_rs, r2a_rs, r2b_rs, z_ss, z_rs, p_ss, p_rs,
):
    dp = lax.axis_index("dp")
    z = lax.axis_index("tensor")
    x = dp // 8
    y = (dp // 2) % 4
    c = dp % 2

    def dev(dx=0, dy=0, dc=0, dz=0):
        return (((x + dx) % 4) * 8 + ((y + dy) % 4) * 2 + (c + dc) % 2, (z + dz) % 4)

    def send(src, dst, ss, rs, target):
        pltpu.make_async_remote_copy(
            src_ref=src, dst_ref=dst, send_sem=ss, recv_sem=rs, device_id=target, device_id_type=MESH
        ).start()

    def wait_all(ref, sem):
        pltpu.make_async_copy(ref, ref, sem).wait()

    barrier = pltpu.get_barrier_semaphore()

    def greet(i, carry):
        pl.semaphore_signal(barrier, inc=1, device_id=dev(i // 8, (i // 2) % 4, i % 2), device_id_type=MESH)
        return carry

    lax.fori_loop(1, 32, greet, 0)
    for dz in range(1, 4):
        pl.semaphore_signal(barrier, inc=1, device_id=dev(dz=dz), device_id_type=MESH)

    def g_copy(k):
        part = pl.ds((k % CH) * 4 * RQ, 4 * RQ)
        return pltpu.make_async_copy(grads.at[k // CH, :, :, :, part, :], graw.at[k], g_sem.at[k])

    ins = [
        pltpu.make_async_copy(a, b, in_sem.at[i])
        for i, (a, b) in enumerate(
            (
                (params, v_params), (moments, v_moms), (row_stat, v_row), (col_stat, v_col), (hidden, v_hid),
                (cell, v_cell), (input_w, v_iw), (recur_w, v_rw), (gate_bias, v_gb), (head_w, v_hw),
                (head_bias, v_hb), (w1, v_w1), (w2, v_w2),
            )
        )
    ]
    for k in range(NC):
        g_copy(k).start()
    for copy in ins:
        copy.start()

    rows = [pl.ds(q * RQ, RQ) for q in range(4)]

    def spread(k, core, write):
        def step(i, carry):
            a, b = i // 4, i % 4
            for q in range(4):
                v = graw[k, a, b, core, rows[q], :].astype(F32)
                write(q, a if q < 2 else b, b if q < 2 else a, v)
            return carry

        lax.fori_loop(0, 16, step, 0)

    def stage_d(k):
        g_copy(k).wait()

        def write(q, i, j, v):
            stage[k, q, i, j] = v

        spread(k, 1 - c, write)
        if k == 0:
            pl.semaphore_wait(barrier, 34)
        send(stage.at[k], acc.at[k], s_sem.at[0], d_rs.at[k], dev(dc=1))

    first = (x, y)
    second = (y, x)
    ways = ((dev(dx=1), dev(dx=3)), (dev(dy=1), dev(dy=3)))

    def stage_1(k):
        wait_all(acc.at[k], d_rs.at[k])

        def write(q, i, j, v):
            acc[k, q, i, j] += v

        spread(k, c, write)
        for h in range(2):
            i0, (plus, minus), qa, qb = first[h], ways[h], 2 * h, 2 * h + 1
            send(acc.at[k, qa, (i0 + 2) % 4], r1a.at[k, qa], s_sem.at[1], r1a_rs.at[k], plus)
            send(acc.at[k, qb, (i0 + 2) % 4], r1a.at[k, qb], s_sem.at[1], r1a_rs.at[k], minus)
        for h in range(2):
            i0, (plus, minus), qa, qb = first[h], ways[h], 2 * h, 2 * h + 1
            send(acc.at[k, qb, (i0 + 1) % 4], r1b.at[k, qb, 0], s_sem.at[2], r1b_rs.at[k], plus)
            send(acc.at[k, qa, (i0 + 3) % 4], r1b.at[k, qa, 1], s_sem.at[2], r1b_rs.at[k], minus)

    def stage_2(k):
        wait_all(r1a.at[k], r1a_rs.at[k])
        for h in range(2):
            i0, (plus, minus), qa, qb = first[h], ways[h], 2 * h, 2 * h + 1
            acc[k, qa, (i0 + 1) % 4] += r1a[k, qa]
            send(acc.at[k, qa, (i0 + 1) % 4], r1b.at[k, qa, 0], s_sem.at[2], r1b_rs.at[k], plus)
            acc[k, qb, (i0 + 3) % 4] += r1a[k, qb]
            send(acc.at[k, qb, (i0 + 3) % 4], r1b.at[k, qb, 1], s_sem.at[2], r1b_rs.at[k], minus)

    def stage_3(k):
        wait_all(r1b.at[k], r1b_rs.at[k])
        for h in range(2):
            i0, j0, (plus, minus), qa, qb = first[h], second[h], ways[1 - h], 2 * h, 2 * h + 1
            for q in (qa, qb):
                acc[k, q, i0] += r1b[k, q, 0] + r1b[k, q, 1]
            send(acc.at[k, qa, i0, (j0 + 2) % 4], r2a.at[k, qa], s_sem.at[3], r2a_rs.at[k], plus)
            send(acc.at[k, qb, i0, (j0 + 2) % 4], r2a.at[k, qb], s_sem.at[3], r2a_rs.at[k], minus)
            send(acc.at[k, qb, i0, (j0 + 1) % 4], r2b.at[k, qb, 0], s_sem.at[4], r2b_rs.at[k], plus)
            send(acc.at[k, qa, i0, (j0 + 3) % 4], r2b.at[k, qa, 1], s_sem.at[4], r2b_rs.at[k], minus)

    def stage_4(k):
        wait_all(r2a.at[k], r2a_rs.at[k])
        for h in range(2):
            i0, j0, (plus, minus), qa, qb = first[h], second[h], ways[1 - h], 2 * h, 2 * h + 1
            acc[k, qa, i0, (j0 + 1) % 4] += r2a[k, qa]
            send(acc.at[k, qa, i0, (j0 + 1) % 4], r2b.at[k, qa, 0], s_sem.at[4], r2b_rs.at[k], plus)
            acc[k, qb, i0, (j0 + 3) % 4] += r2a[k, qb]
            send(acc.at[k, qb, i0, (j0 + 3) % 4], r2b.at[k, qb, 1], s_sem.at[4], r2b_rs.at[k], minus)

    def stage_5(k):
        l = k // CH
        wait_all(r2b.at[k], r2b_rs.at[k])
        for q in range(4):
            h = q // 2
            span = pl.ds((k % CH) * 4 * RQ + q * RQ, RQ)
            g = acc[k, q, first[h], second[h]] + r2b[k, q, 0] + r2b[k, q, 1]
            gsum[l, span, :] = g
            sq = g * g
            rowrep[l, span, :] = jnp.broadcast_to(jnp.sum(sq, 1, keepdims=True), (RQ, 128))
            colacc[l] += jnp.sum(sq.reshape(RQ // 8, 8, CB), 0)
            for n in range(3):
                m = DECAYS[n] * v_moms[n, l, span, :] + (np.float32(1) - DECAYS[n]) * g
                n_moms[n, l, span, :] = m
                macc[l, n] += jnp.sum((m * m).reshape(RQ // 8, 8, CB), 0)
        if k % CH == CH - 1:
            for n in range(3):
                out_copy(n_moms.at[n, l], o_moms.at[n, l], 3 * l + n).start()

    def out_copy(src, dst, i):
        return pltpu.make_async_copy(src, dst, out_sem.at[i])

    lane = lax.broadcasted_iota(jnp.int32, (1, 128), 1)

    def prepare():
        for copy in ins:
            copy.wait()
        colacc[...] = jnp.zeros_like(colacc)
        macc[...] = jnp.zeros_like(macc)
        for l in range(L):
            def square(i, s):
                v = v_params[l, pl.ds(pl.multiple_of(i * 8, 8), 8), :]
                return s + v * v

            pacc[l] = lax.fori_loop(0, RB // 8, square, jnp.zeros((8, CB), F32))
        reps = [jnp.concatenate([lane_to_rows(v_hid[l:l + 1, i * 128:(i + 1) * 128]) for i in range(4)], 0) for l in range(L)]
        for l in range(L):
            mod[l] = reps[l]

        def recur(i, sums):
            at = pl.ds(pl.multiple_of(i * 8, 8), 8)
            w = v_rw[at, :]
            return tuple(sums[l] + w * jnp.tile(mod[l, at, :], (1, 16)) for l in range(L))

        sums = lax.fori_loop(0, H // 8, recur, tuple(jnp.zeros((8, 4 * H), F32) for _ in range(L)))
        for l in range(L):
            pre[l] = jnp.sum(sums[l], 0, keepdims=True) + v_gb[...]
        for i in range(4):
            part = v_hw[i * 128:(i + 1) * 128, :]
            part = jnp.concatenate([part, jnp.zeros((128, 126 - HID), F32)], 1)
            headt[:, i * 128:(i + 1) * 128] = jnp.transpose(part)[0:40, :]
        hbcol[...] = lane_to_rows(jnp.concatenate([v_hb[...], jnp.zeros((1, 126 - HID), F32)], 1))[0:40, :]
        w1t = jnp.concatenate([v_w1[...], jnp.zeros((128 - NF, HID), F32)], 0)
        w1t = jnp.transpose(jnp.concatenate([w1t, jnp.zeros((128, 128 - HID), F32)], 1))[0:HID, :]
        at = lax.broadcasted_iota(jnp.int32, (HID, 256), 1)
        wide = jnp.zeros((HID, 256), F32)
        for n in range(NF):
            hit = ((at // 8) % NF == n) & (at < 144)
            wide = jnp.where(hit, jnp.broadcast_to(w1t[:, n:n + 1], (HID, 256)), wide)
        tall = jnp.broadcast_to(wide[:, None, :], (HID, 8, 256)).reshape(HID * 8, 256)
        tall_at = lax.broadcasted_iota(jnp.int32, (HID * 8, 256), 1)
        tall_row = lax.broadcasted_iota(jnp.int32, (HID * 8, 256), 0)
        tall = jnp.where(tall_at % 8 == tall_row % 8, tall, 0.0)
        high = tall.astype(BF16).astype(F32)
        wst[...] = jnp.where(tall_at < 96, high, tall - high).astype(BF16)
        for o in range(2):
            w2rep[o] = jnp.broadcast_to(v_w2[:, o:o + 1], (HID, 128))

    def total(v):
        return jnp.sum(jnp.sum(v, 0, keepdims=True), 1, keepdims=True)

    def put(values):
        row = jnp.zeros((1, 128), F32)
        for j, v in enumerate(values):
            row = jnp.where(lane == j, v, row)
        return row

    def pick(row, j):
        return jnp.sum(jnp.where(lane == j, row, 0.0), 1, keepdims=True)

    def z_send(l):
        for i in range(2):
            zs[l, :, i * 128:(i + 1) * 128] = rows_to_lane(rowrep[l, i * 128:(i + 1) * 128, :])
        zs[l, :, 256:384] = put([total(colacc[l]), total(macc[l, 0]), total(macc[l, 1]), total(macc[l, 2]), total(pacc[l])])
        for dz in range(1, 4):
            send(zs.at[l], zr.at[l, dz - 1], z_ss.at[l], z_rs.at[l], dev(dz=dz))

    def p_send(l):
        wait_all(zr.at[l], z_rs.at[l])
        got = zs[l] + zr[l, 0] + zr[l, 1] + zr[l, 2]
        new = 0.9 * v_row[l:l + 1, :] + 0.1 * got[:, 0:256] / KV
        n_rows[l:l + 1, :] = new
        ps[l, :, 0:256] = jnp.sum(colacc[l], 0, keepdims=True)
        ps[l, :, 256:384] = got[:, 256:384] + jnp.where(lane == 5, jnp.sum(new, 1, keepdims=True), 0.0)

        def out(i, carry):
            send(ps.at[l], pr.at[l, i - 1], p_ss.at[l], p_rs.at[l], dev(i // 8, (i // 2) % 4, i % 2))
            return carry

        lax.fori_loop(1, 32, out, 0)
        for i in range(2):
            rowrep[l, i * 128:(i + 1) * 128, :] = lane_to_rows(new[:, i * 128:(i + 1) * 128])

    def control(l):
        wait_all(pr.at[l], p_rs.at[l])
        got = ps[l] + jnp.sum(pr[l], 0)
        new = 0.9 * v_col[l:l + 1, :] + 0.1 * got[:, 0:256] / D
        n_cols[l:l + 1, :] = new
        sums = got[:, 256:384]
        means = sums / (D * KV)
        stats = jnp.log(means + 1e-06)
        gates = pre[l]
        for j in range(5):
            gates = gates + pick(stats, j) * v_iw[j:j + 1, :]
        i_g = jax.nn.sigmoid(gates[:, 0:H])
        f_g = jax.nn.sigmoid(gates[:, H:2 * H])
        c_g = jnp.tanh(gates[:, 2 * H:3 * H])
        o_g = jax.nn.sigmoid(gates[:, 3 * H:])
        new_cell = f_g * v_cell[l:l + 1, :] + i_g * c_g
        new_hid = o_g * jnp.tanh(new_cell)
        n_cell[l:l + 1, :] = new_cell
        n_hid[l:l + 1, :] = new_hid
        m = jnp.sum(headt[...] * new_hid, 1, keepdims=True) + hbcol[...]
        mod[l, 0:40, :] = m
        mod[l, 32:33, :] = jnp.exp(m[32:33, :])
        mod[l, 33:34, :] = 0.5 * m[33:34, :]
        row_mean = pick(sums, 5) / D
        colrow[l] = new / row_mean
        norms[l] = jnp.broadcast_to(
            jnp.where(lane == 0, lax.rsqrt(pick(means, 4) + 1e-06), lax.rsqrt(pick(means, 0) + 1e-06)), (1, 128)
        )

    def network(l, begin, end):
        def step(i, carry):
            at = pl.ds(pl.multiple_of(i * 8, 8), 8)
            g = gsum[l, at, :]
            p = v_params[l, at, :]
            scale = lax.rsqrt(jnp.tile(rowrep[l, at, :], (1, 2)) * colrow[l] + 1e-08)
            p_norm = pick(norms[l], 0)
            g_norm = pick(norms[l], 1)
            ins = jnp.concatenate(
                [g * scale] + [n_moms[n, l, at, :] * scale for n in range(3)] + [p * p_norm, g * g_norm], 0
            )
            high = ins.astype(BF16)
            low = (ins - high.astype(F32)).astype(BF16)
            units = jnp.dot(
                wst[:, 0:144], jnp.concatenate([high, low, high], 0), preferred_element_type=F32
            )
            direction = jnp.zeros((8, CB), F32)
            magnitude = jnp.zeros((8, CB), F32)
            for h in range(HID):
                u = jnp.maximum(units[h * 8:(h + 1) * 8, :] + jnp.tile(mod[l, h:h + 1, :], (1, 2)), 0.0)
                direction = direction + jnp.tile(w2rep[0, h:h + 1, :], (1, 2)) * u
                magnitude = magnitude + jnp.tile(w2rep[1, h:h + 1, :], (1, 2)) * u
            rate = jnp.tile(mod[l, 32:33, :], (1, 2))
            gain = jnp.tile(mod[l, 33:34, :], (1, 2))
            n_params[l, at, :] = p - rate * direction * jnp.exp(gain * magnitude)
            return carry

        lax.fori_loop(begin, end, step, 0)

    stage_d(0)
    stage_d(1)
    for t in range(NC + 4):
        if t < NC:
            stage_1(t)
        if t + 2 < NC:
            stage_d(t + 2)
        if 0 <= t - 1 < NC:
            stage_2(t - 1)
        if t == 1:
            prepare()
        if 0 <= t - 2 < NC:
            stage_3(t - 2)
        if 0 <= t - 3 < NC:
            stage_4(t - 3)
        if 0 <= t - 4 < NC:
            stage_5(t - 4)
        if t == CH + 3:
            z_send(0)
        if t == CH + 4:
            p_send(0)
        if t == CH + 5:
            control(0)
    z_send(1)
    network(0, 0, 16)
    p_send(1)
    network(0, 16, 32)
    outs = [
        out_copy(n_params.at[0], o_params.at[0], 6),
        out_copy(n_params.at[1], o_params.at[1], 7),
        out_copy(n_rows, o_rows, 8),
        out_copy(n_cols, o_cols, 9),
        out_copy(n_hid, o_hid, 10),
        out_copy(n_cell, o_cell, 11),
    ]
    outs[0].start()
    outs[2].start()
    control(1)
    for i in (3, 4, 5):
        outs[i].start()
    network(1, 0, 32)
    outs[1].start()
    for l in range(L):
        for n in range(3):
            out_copy(n_moms.at[n, l], o_moms.at[n, l], 3 * l + n).wait()
    wait_all(acc, s_sem.at[0])
    wait_all(r1a, s_sem.at[1])
    wait_all(r1b, s_sem.at[2])
    wait_all(r2a, s_sem.at[3])
    wait_all(r2b, s_sem.at[4])
    for l in range(L):
        wait_all(zr.at[l], z_ss.at[l])
        wait_all(pr.at[l], p_ss.at[l])
    for copy in outs:
        copy.wait()


def body(grads, params, moments, row_stat, col_stat, hidden, cell, input_w, recur_w, gate_bias, head_w, head_bias, w1, w2):
    any_space = pl.BlockSpec(memory_space=pl.ANY)
    vmem = pltpu.VMEM
    dma = pltpu.SemaphoreType.DMA
    quarter = (RQ, CB)
    return pl.pallas_call(
        kernel,
        out_shape=(
            jax.ShapeDtypeStruct((L, RB, CB), F32),
            jax.ShapeDtypeStruct((3, L, RB, CB), F32),
            jax.ShapeDtypeStruct((L, RB), F32),
            jax.ShapeDtypeStruct((L, CB), F32),
            jax.ShapeDtypeStruct((L, H), F32),
            jax.ShapeDtypeStruct((L, H), F32),
        ),
        in_specs=[any_space] * 14,
        out_specs=(any_space,) * 6,
        scratch_shapes=[
            vmem((NC, 4, 4, 2, 4 * RQ, CB), BF16),
            vmem((NC, 4, 4, 4) + quarter, F32),
            vmem((NC, 4, 4, 4) + quarter, F32),
            vmem((NC, 4, 4) + quarter, F32),
            vmem((NC, 4, 2, 4) + quarter, F32),
            vmem((NC, 4) + quarter, F32),
            vmem((NC, 4, 2) + quarter, F32),
            vmem((L, RB, CB), F32),
            vmem((3, L, RB, CB), F32),
            vmem((L, RB), F32),
            vmem((L, CB), F32),
            vmem((L, H), F32),
            vmem((L, H), F32),
            vmem((5, 4 * H), F32),
            vmem((H, 4 * H), F32),
            vmem((1, 4 * H), F32),
            vmem((H, HID + 2), F32),
            vmem((1, HID + 2), F32),
            vmem((NF, HID), F32),
            vmem((HID, 2), F32),
            vmem((L, RB, CB), F32),
            vmem((3, L, RB, CB), F32),
            vmem((L, RB), F32),
            vmem((L, CB), F32),
            vmem((L, H), F32),
            vmem((L, H), F32),
            vmem((L, RB, CB), F32),
            vmem((L, RB, 128), F32),
            vmem((L, 8, CB), F32),
            vmem((L, 3, 8, CB), F32),
            vmem((L, 8, CB), F32),
            vmem((L, 1, 4 * H), F32),
            vmem((40, H), F32),
            vmem((40, 128), F32),
            vmem((HID * 8, 256), BF16),
            vmem((2, HID, 128), F32),
            vmem((L, 1, 384), F32),
            vmem((L, 3, 1, 384), F32),
            vmem((L, 1, 384), F32),
            vmem((L, 31, 1, 384), F32),
            vmem((L, H, 128), F32),
            vmem((L, 1, 128), F32),
            vmem((L, 1, CB), F32),
            dma((13,)),
            dma((NC,)),
            dma((12,)),
            dma((5,)),
            dma((NC,)),
            dma((NC,)),
            dma((NC,)),
            dma((NC,)),
            dma((NC,)),
            dma((L,)),
            dma((L,)),
            dma((L,)),
            dma((L,)),
        ],
        compiler_params=pltpu.CompilerParams(
            collective_id=0, has_side_effects=True, vmem_limit_bytes=60 * 2**20
        ),
        name="update",
    )(
        grads.reshape(L, 4, 4, 2, RB, CB), params, moments, row_stat, col_stat, hidden, cell, input_w, recur_w,
        gate_bias.reshape(1, 4 * H), head_w, head_bias.reshape(1, HID + 2), w1, w2,
    )


def solution(mesh):
    return jax.shard_map(
        body,
        mesh=mesh,
        in_specs=(
            P("dp", None, None, "tensor"),
            P(None, "dp", "tensor"),
            P(None, None, "dp", "tensor"),
            P(None, "dp"),
            P(None, "tensor"),
        )
        + (P(),) * 9,
        out_specs=(
            P(None, "dp", "tensor"),
            P(None, None, "dp", "tensor"),
            P(None, "dp"),
            P(None, "tensor"),
            P(),
            P(),
        ),
        check_vma=False,
    )
```

```python
import functools

import jax
import jax.numpy as jnp
import numpy as np
from jax import lax
from jax.experimental import pallas as pl
from jax.experimental.pallas import tpu as pltpu
from jax.sharding import PartitionSpec as P

D = 8192
KV = 1024
L = 2
H = 512
HID = 32
NF = 6
AHEAD = 2
CH = 4
NC = L * CH
RB = 256
CB = 256
RQ = RB // CH // 4
MESH = pl.DeviceIdType.MESH
F32 = jnp.float32
BF16 = jnp.bfloat16
DECAYS = tuple(np.float32(v) for v in (0.5, 0.9, 0.99))


def lane_to_rows(row):
    return jnp.transpose(jnp.broadcast_to(row, (128, 128)))


def rows_to_lane(block):
    return jnp.transpose(block)[0:1, :]


def twice(v):
    return jnp.concatenate([v, v], 1)


def network(begin, end, g_ref, m_refs, p_ref, row_ref, col_ref, norm_ref, wst_ref, w2_ref, mod_ref, out_ref):
    ones = jnp.where(lax.broadcasted_iota(jnp.int32, (16, CB), 0) < 2, 1.0, 0.0).astype(BF16)

    def tile(at):
        g = g_ref[at, :]
        p = p_ref[at, :]
        scale = lax.rsqrt(twice(row_ref[at, :]) * col_ref[...] + 1e-08)
        ins = [g * scale] + [m[at, :] * scale for m in m_refs]
        ins += [p * twice(norm_ref[0:1, :]), g * twice(norm_ref[1:2, :])]
        ins = jnp.concatenate(ins, 0)
        high = ins.astype(BF16)
        low = (ins - high.astype(F32)).astype(BF16)
        units = jnp.dot(
            wst_ref[:, 0:160], jnp.concatenate([high, low, high, ones], 0), preferred_element_type=F32
        )
        direction = jnp.zeros((8, CB), F32)
        magnitude = jnp.zeros((8, CB), F32)
        for h in range(HID):
            u = jnp.maximum(units[h * 8:(h + 1) * 8, :], 0.0)
            direction = direction + twice(w2_ref[0, h:h + 1, :]) * u
            magnitude = magnitude + twice(w2_ref[1, h:h + 1, :]) * u
        rate = twice(mod_ref[HID:HID + 1, :])
        gain = twice(mod_ref[HID + 1:HID + 2, :])
        out_ref[at, :] = p - rate * direction * jnp.exp(gain * magnitude)

    def step(i, carry):
        for u in range(8):
            tile(pl.ds(pl.multiple_of(i * 64 + u * 8, 8), 8))
        return carry

    lax.fori_loop(begin, end, step, 0)


def kernel(
    grads, params, moments, row_stat, col_stat, hidden, cell, input_w, recur_w, gate_bias, head_w, head_bias, w1, w2,
    n_params, n_moms, v_params, gsum, rowrep, colrow, norms, wst, w2rep, mod, n_rows, n_cols, n_hid, n_cell,
    graw, stage, acc, r1a, r1b, r2a, r2b,
    v_moms, v_row, v_col, v_hid, v_cell, v_iw, v_rw, v_gb, headt, v_hb, v_w1, v_w2,
    hidrep, colacc, macc, pacc, pre, hbcol, zs, zr, ps, pr,
    in_sem, g_sem, s_sem, d_rs, r1a_rs, r1b_rs, r2a_rs, r2b_rs, z_ss, z_rs, p_ss, p_rs,
):
    dp = lax.axis_index("dp")
    z = lax.axis_index("tensor")
    x = dp // 8
    y = (dp // 2) % 4
    c = dp % 2

    def dev(dx=0, dy=0, dc=0, dz=0):
        return (((x + dx) % 4) * 8 + ((y + dy) % 4) * 2 + (c + dc) % 2, (z + dz) % 4)

    def send(src, dst, ss, rs, target):
        pltpu.make_async_remote_copy(
            src_ref=src, dst_ref=dst, send_sem=ss, recv_sem=rs, device_id=target, device_id_type=MESH
        ).start()

    def wait_all(ref, sem):
        pltpu.make_async_copy(ref, ref, sem).wait()

    def g_copy(k):
        part = pl.ds((k % CH) * 4 * RQ, 4 * RQ)
        return pltpu.make_async_copy(grads.at[k // CH, :, :, :, part, :], graw.at[k], g_sem.at[k])

    for k in range(AHEAD):
        g_copy(k).start()
    barrier = pltpu.get_barrier_semaphore()

    def greet(i, carry):
        pl.semaphore_signal(barrier, inc=1, device_id=dev(i // 8, (i // 2) % 4, i % 2), device_id_type=MESH)
        return carry

    lax.fori_loop(1, 32, greet, 0)
    for dz in range(1, 4):
        pl.semaphore_signal(barrier, inc=1, device_id=dev(dz=dz), device_id_type=MESH)

    ins = [
        pltpu.make_async_copy(a, b, in_sem.at[i])
        for i, (a, b) in enumerate(
            (
                (params, v_params), (moments, v_moms), (row_stat, v_row), (col_stat, v_col), (hidden, v_hid),
                (cell, v_cell), (input_w, v_iw), (recur_w, v_rw), (gate_bias, v_gb), (head_w, headt),
                (head_bias, v_hb), (w1, v_w1), (w2, v_w2),
            )
        )
    ]
    def load_more(k):
        if k + AHEAD < NC:
            g_copy(k + AHEAD).start()
        if k == 1:
            for copy in ins:
                copy.start()

    def spread(k, core, write):
        def step(i, carry):
            a, b = i // 4, i % 4
            v = graw[k, a, b, core].astype(F32)
            for q in range(4):
                write(q, a if q < 2 else b, b if q < 2 else a, v[q * RQ:(q + 1) * RQ, :])
            return carry

        lax.fori_loop(0, 16, step, 0)

    def stage_d(k):
        g_copy(k).wait()
        load_more(k)

        def write(q, i, j, v):
            stage[k, q, i, j] = v

        spread(k, 1 - c, write)
        if k == 0:
            pl.semaphore_wait(barrier, 34)
        send(stage.at[k], acc.at[k], s_sem.at[0], d_rs.at[k], dev(dc=1))

    first = (x, y)
    second = (y, x)
    ways = ((dev(dx=1), dev(dx=3)), (dev(dy=1), dev(dy=3)))

    def stage_1(k):
        wait_all(acc.at[k], d_rs.at[k])

        def write(q, i, j, v):
            acc[k, q, i, j] += v

        spread(k, c, write)
        for h in range(2):
            i0, (plus, minus), qa, qb = first[h], ways[h], 2 * h, 2 * h + 1
            send(acc.at[k, qa, (i0 + 2) % 4], r1a.at[k, qa], s_sem.at[1], r1a_rs.at[k], plus)
            send(acc.at[k, qb, (i0 + 2) % 4], r1a.at[k, qb], s_sem.at[1], r1a_rs.at[k], minus)
        for h in range(2):
            i0, (plus, minus), qa, qb = first[h], ways[h], 2 * h, 2 * h + 1
            send(acc.at[k, qb, (i0 + 1) % 4], r1b.at[k, qb, 0], s_sem.at[2], r1b_rs.at[k], plus)
            send(acc.at[k, qa, (i0 + 3) % 4], r1b.at[k, qa, 1], s_sem.at[2], r1b_rs.at[k], minus)

    def stage_2(k):
        wait_all(r1a.at[k], r1a_rs.at[k])
        for h in range(2):
            i0, (plus, minus), qa, qb = first[h], ways[h], 2 * h, 2 * h + 1
            acc[k, qa, (i0 + 1) % 4] += r1a[k, qa]
            send(acc.at[k, qa, (i0 + 1) % 4], r1b.at[k, qa, 0], s_sem.at[2], r1b_rs.at[k], plus)
            acc[k, qb, (i0 + 3) % 4] += r1a[k, qb]
            send(acc.at[k, qb, (i0 + 3) % 4], r1b.at[k, qb, 1], s_sem.at[2], r1b_rs.at[k], minus)

    def stage_3(k):
        wait_all(r1b.at[k], r1b_rs.at[k])
        for h in range(2):
            i0, j0, (plus, minus), qa, qb = first[h], second[h], ways[1 - h], 2 * h, 2 * h + 1
            for q in (qa, qb):
                acc[k, q, i0] += r1b[k, q, 0] + r1b[k, q, 1]
            send(acc.at[k, qa, i0, (j0 + 2) % 4], r2a.at[k, qa], s_sem.at[3], r2a_rs.at[k], plus)
            send(acc.at[k, qb, i0, (j0 + 2) % 4], r2a.at[k, qb], s_sem.at[3], r2a_rs.at[k], minus)
            send(acc.at[k, qb, i0, (j0 + 1) % 4], r2b.at[k, qb, 0], s_sem.at[4], r2b_rs.at[k], plus)
            send(acc.at[k, qa, i0, (j0 + 3) % 4], r2b.at[k, qa, 1], s_sem.at[4], r2b_rs.at[k], minus)

    def stage_4(k):
        wait_all(r2a.at[k], r2a_rs.at[k])
        for h in range(2):
            i0, j0, (plus, minus), qa, qb = first[h], second[h], ways[1 - h], 2 * h, 2 * h + 1
            acc[k, qa, i0, (j0 + 1) % 4] += r2a[k, qa]
            send(acc.at[k, qa, i0, (j0 + 1) % 4], r2b.at[k, qa, 0], s_sem.at[4], r2b_rs.at[k], plus)
            acc[k, qb, i0, (j0 + 3) % 4] += r2a[k, qb]
            send(acc.at[k, qb, i0, (j0 + 3) % 4], r2b.at[k, qb, 1], s_sem.at[4], r2b_rs.at[k], minus)

    def stage_5(k):
        l = k // CH
        wait_all(r2b.at[k], r2b_rs.at[k])
        for q in range(4):
            h = q // 2
            span = pl.ds((k % CH) * 4 * RQ + q * RQ, RQ)
            g = acc[k, q, first[h], second[h]] + r2b[k, q, 0] + r2b[k, q, 1]
            gsum[l, span, :] = g
            sq = g * g
            rowrep[l, span, :] = jnp.broadcast_to(jnp.sum(sq, 1, keepdims=True), (RQ, 128))
            colacc[l] += jnp.sum(sq.reshape(RQ // 8, 8, CB), 0)
            for n in range(3):
                m = DECAYS[n] * v_moms[n, l, span, :] + (np.float32(1) - DECAYS[n]) * g
                n_moms[n, l, span, :] = m
                macc[l, n] += jnp.sum((m * m).reshape(RQ // 8, 8, CB), 0)

    lane = lax.broadcasted_iota(jnp.int32, (1, 128), 1)

    def prepare():
        for copy in ins:
            copy.wait()
        colacc[...] = jnp.zeros_like(colacc)
        macc[...] = jnp.zeros_like(macc)
        for l in range(L):
            def square(i, s):
                v = v_params[l, pl.ds(pl.multiple_of(i * 8, 8), 8), :]
                return s + v * v

            pacc[l] = lax.fori_loop(0, RB // 8, square, jnp.zeros((8, CB), F32))
        reps = [jnp.concatenate([lane_to_rows(v_hid[l:l + 1, i * 128:(i + 1) * 128]) for i in range(4)], 0) for l in range(L)]
        for l in range(L):
            hidrep[l] = reps[l]

        def recur(i, sums):
            at = pl.ds(pl.multiple_of(i * 8, 8), 8)
            w = v_rw[at, :]
            return tuple(sums[l] + w * jnp.tile(hidrep[l, at, :], (1, 16)) for l in range(L))

        sums = lax.fori_loop(0, H // 8, recur, tuple(jnp.zeros((8, 4 * H), F32) for _ in range(L)))
        for l in range(L):
            pre[l] = jnp.sum(sums[l], 0, keepdims=True) + v_gb[...]
        hbcol[...] = lane_to_rows(jnp.concatenate([v_hb[...], jnp.zeros((1, 126 - HID), F32)], 1))[0:HID + 2, :]
        w1t = jnp.concatenate([v_w1[...], jnp.zeros((128 - NF, HID), F32)], 0)
        w1t = jnp.transpose(jnp.concatenate([w1t, jnp.zeros((128, 128 - HID), F32)], 1))[0:HID, :]
        at = lax.broadcasted_iota(jnp.int32, (HID, 256), 1)
        wide = jnp.zeros((HID, 256), F32)
        for n in range(NF):
            hit = ((at // 8) % NF == n) & (at < 144)
            wide = jnp.where(hit, jnp.broadcast_to(w1t[:, n:n + 1], (HID, 256)), wide)
        tall = jnp.broadcast_to(wide[:, None, :], (HID, 8, 256)).reshape(HID * 8, 256)
        tall_at = lax.broadcasted_iota(jnp.int32, (HID * 8, 256), 1)
        tall_row = lax.broadcasted_iota(jnp.int32, (HID * 8, 256), 0)
        tall = jnp.where(tall_at % 8 == tall_row % 8, tall, 0.0)
        high = tall.astype(BF16).astype(F32)
        tall = jnp.where(tall_at < 96, high, tall - high).astype(BF16)
        for l in range(L):
            wst[l] = tall
        for o in range(2):
            row = jnp.concatenate([v_w2[o:o + 1, :], jnp.zeros((1, 128 - HID), F32)], 1)
            w2rep[o] = lane_to_rows(row)[0:HID, :]

    def total(v):
        return jnp.sum(jnp.sum(v, 0, keepdims=True), 1, keepdims=True)

    def put(values):
        row = jnp.zeros((1, 128), F32)
        for j, v in enumerate(values):
            row = jnp.where(lane == j, v, row)
        return row

    def pick(row, j):
        return jnp.sum(jnp.where(lane == j, row, 0.0), 1, keepdims=True)

    def z_send(l):
        for i in range(2):
            zs[l, :, i * 128:(i + 1) * 128] = rows_to_lane(rowrep[l, i * 128:(i + 1) * 128, :])
        zs[l, :, 256:384] = put([total(colacc[l]), total(macc[l, 0]), total(macc[l, 1]), total(macc[l, 2]), total(pacc[l])])
        for dz in range(1, 4):
            send(zs.at[l], zr.at[l, dz - 1], z_ss.at[l], z_rs.at[l], dev(dz=dz))

    def p_send(l):
        wait_all(zr.at[l], z_rs.at[l])
        got = zs[l] + zr[l, 0] + zr[l, 1] + zr[l, 2]
        new = 0.9 * v_row[l:l + 1, :] + 0.1 * got[:, 0:256] / KV
        n_rows[l:l + 1, :] = new
        ps[l, :, 0:256] = jnp.sum(colacc[l], 0, keepdims=True)
        ps[l, :, 256:384] = got[:, 256:384] + jnp.where(lane == 5, jnp.sum(new, 1, keepdims=True), 0.0)

        def out(i, carry):
            send(ps.at[l], pr.at[l, i - 1], p_ss.at[l], p_rs.at[l], dev(i // 8, (i // 2) % 4, i % 2))
            return carry

        lax.fori_loop(1, 32, out, 0)
        for i in range(2):
            rowrep[l, i * 128:(i + 1) * 128, :] = lane_to_rows(new[:, i * 128:(i + 1) * 128])

    def control(l):
        wait_all(pr.at[l], p_rs.at[l])
        got = ps[l] + jnp.sum(pr[l], 0)
        new = 0.9 * v_col[l:l + 1, :] + 0.1 * got[:, 0:256] / D
        n_cols[l:l + 1, :] = new
        sums = got[:, 256:384]
        means = sums / (D * KV)
        stats = jnp.log(means + 1e-06)
        gates = pre[l]
        for j in range(5):
            gates = gates + pick(stats, j) * v_iw[j:j + 1, :]
        i_g = jax.nn.sigmoid(gates[:, 0:H])
        f_g = jax.nn.sigmoid(gates[:, H:2 * H])
        c_g = jnp.tanh(gates[:, 2 * H:3 * H])
        o_g = jax.nn.sigmoid(gates[:, 3 * H:])
        new_cell = f_g * v_cell[l:l + 1, :] + i_g * c_g
        new_hid = o_g * jnp.tanh(new_cell)
        n_cell[l:l + 1, :] = new_cell
        n_hid[l:l + 1, :] = new_hid
        m = jnp.sum(headt[...] * new_hid, 1, keepdims=True) + hbcol[...]
        mod[l, 0:HID + 2, :] = jnp.broadcast_to(m, (HID + 2, 128))
        mod[l, HID:HID + 1, :] = jnp.broadcast_to(jnp.exp(m[HID:HID + 1, :]), (1, 128))
        mod[l, HID + 1:HID + 2, :] = jnp.broadcast_to(0.5 * m[HID + 1:HID + 2, :], (1, 128))
        bias = jnp.broadcast_to(m[0:HID, None, :], (HID, 8, 128)).reshape(HID * 8, 128)
        high = bias.astype(BF16).astype(F32)
        side = wst[l, :, 128:256].astype(F32)
        side = jnp.where(lane == 16, high, jnp.where(lane == 17, bias - high, side))
        wst[l, :, 128:256] = side.astype(BF16)
        row_mean = pick(sums, 5) / D
        colrow[l] = new / row_mean
        norms[l, 0:1, :] = jnp.broadcast_to(lax.rsqrt(pick(means, 4) + 1e-06), (1, 128))
        norms[l, 1:2, :] = jnp.broadcast_to(lax.rsqrt(pick(means, 0) + 1e-06), (1, 128))

    def network_0(begin, end):
        network(
            begin, end, gsum.at[0], [n_moms.at[n, 0] for n in range(3)], v_params.at[0], rowrep.at[0], colrow.at[0],
            norms.at[0], wst.at[0], w2rep, mod.at[0], n_params,
        )

    stage_d(0)
    stage_d(1)
    for t in range(NC + 4):
        if t < NC:
            stage_1(t)
        if t + 2 < NC:
            stage_d(t + 2)
        if 0 <= t - 1 < NC:
            stage_2(t - 1)
        if t == 1:
            prepare()
        if 0 <= t - 2 < NC:
            stage_3(t - 2)
        if 0 <= t - 3 < NC:
            stage_4(t - 3)
        if 0 <= t - 4 < NC:
            stage_5(t - 4)
        if t == CH + 3:
            z_send(0)
        if t == CH + 4:
            p_send(0)
        if t == CH + 5:
            control(0)
    z_send(1)
    network_0(0, 2)
    p_send(1)
    network_0(2, 4)
    control(1)
    wait_all(acc, s_sem.at[0])
    wait_all(r1a, s_sem.at[1])
    wait_all(r1b, s_sem.at[2])
    wait_all(r2a, s_sem.at[3])
    wait_all(r2b, s_sem.at[4])
    for l in range(L):
        wait_all(zr.at[l], z_ss.at[l])
        wait_all(pr.at[l], p_ss.at[l])


def finish(
    params_0, moms, params, gsum, rowrep, colrow, norms, wst, w2rep, mod, rows, cols, hid, cell,
    o_params, o_moms, o_rows, o_cols, o_hid, o_cell, params_1, sem,
):
    copies = [
        pltpu.make_async_copy(a, b, sem.at[i])
        for i, (a, b) in enumerate(
            ((moms, o_moms), (params_0, o_params.at[0]), (rows, o_rows), (cols, o_cols), (hid, o_hid), (cell, o_cell))
        )
    ]
    for copy in copies:
        copy.start()
    for part in range(2):
        network(
            2 * part, 2 * part + 2, gsum.at[1], [moms.at[n, 1] for n in range(3)], params.at[1], rowrep.at[1],
            colrow.at[1], norms.at[1], wst.at[1], w2rep, mod.at[1], params_1,
        )
        half = pl.ds(part * RB // 2, RB // 2)
        copy = pltpu.make_async_copy(params_1.at[half, :], o_params.at[1, half, :], sem.at[6 + part])
        copy.start()
        copies.append(copy)
    for copy in copies:
        copy.wait()


def body(grads, params, moments, row_stat, col_stat, hidden, cell, input_w, recur_w, gate_bias, head_w, head_bias, w1, w2):
    hbm = pl.BlockSpec(memory_space=pltpu.HBM)
    held = pl.BlockSpec(memory_space=pltpu.VMEM)
    vmem = pltpu.VMEM
    dma = pltpu.SemaphoreType.DMA
    quarter = (RQ, CB)
    between = (
        vmem((RB, CB), F32),
        vmem((3, L, RB, CB), F32),
        vmem((L, RB, CB), F32),
        vmem((L, RB, CB), F32),
        vmem((L, RB, 128), F32),
        vmem((L, 1, CB), F32),
        vmem((L, 2, 128), F32),
        vmem((L, HID * 8, 256), BF16),
        vmem((2, HID, 128), F32),
        vmem((L, HID + 2, 128), F32),
        vmem((L, RB), F32),
        vmem((L, CB), F32),
        vmem((L, H), F32),
        vmem((L, H), F32),
    )
    operands = (
        grads.reshape(L, 4, 4, 2, RB, CB), params, moments, row_stat, col_stat, hidden, cell, input_w, recur_w,
        gate_bias.reshape(1, 4 * H), head_w.T, head_bias.reshape(1, HID + 2), w1, w2.T,
    )
    results = pl.pallas_call(
        kernel,
        out_shape=between,
        in_specs=[hbm] * 14,
        out_specs=(held,) * len(between),
        scratch_shapes=[
            vmem((NC, 4, 4, 2, 4 * RQ, CB), BF16),
            vmem((NC, 4, 4, 4) + quarter, F32),
            vmem((NC, 4, 4, 4) + quarter, F32),
            vmem((NC, 4, 4) + quarter, F32),
            vmem((NC, 4, 2, 4) + quarter, F32),
            vmem((NC, 4) + quarter, F32),
            vmem((NC, 4, 2) + quarter, F32),
            vmem((3, L, RB, CB), F32),
            vmem((L, RB), F32),
            vmem((L, CB), F32),
            vmem((L, H), F32),
            vmem((L, H), F32),
            vmem((5, 4 * H), F32),
            vmem((H, 4 * H), F32),
            vmem((1, 4 * H), F32),
            vmem((HID + 2, H), F32),
            vmem((1, HID + 2), F32),
            vmem((NF, HID), F32),
            vmem((2, HID), F32),
            vmem((L, H, 128), F32),
            vmem((L, 8, CB), F32),
            vmem((L, 3, 8, CB), F32),
            vmem((L, 8, CB), F32),
            vmem((L, 1, 4 * H), F32),
            vmem((HID + 2, 128), F32),
            vmem((L, 1, 384), F32),
            vmem((L, 3, 1, 384), F32),
            vmem((L, 1, 384), F32),
            vmem((L, 31, 1, 384), F32),
            dma((13,)),
            dma((NC,)),
            dma((5,)),
            dma((NC,)),
            dma((NC,)),
            dma((NC,)),
            dma((NC,)),
            dma((NC,)),
            dma((L,)),
            dma((L,)),
            dma((L,)),
            dma((L,)),
        ],
        compiler_params=pltpu.CompilerParams(
            collective_id=0, has_side_effects=True, vmem_limit_bytes=46 * 2**20
        ),
        name="update",
    )(*[pltpu.with_memory_space_constraint(v, pltpu.HBM) for v in operands])
    return pl.pallas_call(
        finish,
        out_shape=(
            jax.ShapeDtypeStruct((L, RB, CB), F32),
            jax.ShapeDtypeStruct((3, L, RB, CB), F32),
            jax.ShapeDtypeStruct((L, RB), F32),
            jax.ShapeDtypeStruct((L, CB), F32),
            jax.ShapeDtypeStruct((L, H), F32),
            jax.ShapeDtypeStruct((L, H), F32),
        ),
        in_specs=[held] * len(between),
        out_specs=(hbm,) * 6,
        scratch_shapes=[vmem((RB, CB), F32), dma((8,))],
        compiler_params=pltpu.CompilerParams(vmem_limit_bytes=16 * 2**20),
        name="finish",
    )(*results)


def solution(mesh):
    return jax.shard_map(
        body,
        mesh=mesh,
        in_specs=(
            P("dp", None, None, "tensor"),
            P(None, "dp", "tensor"),
            P(None, None, "dp", "tensor"),
            P(None, "dp"),
            P(None, "tensor"),
        )
        + (P(),) * 9,
        out_specs=(
            P(None, "dp", "tensor"),
            P(None, None, "dp", "tensor"),
            P(None, "dp"),
            P(None, "tensor"),
            P(),
            P(),
        ),
        check_vma=False,
    )
```

```python
import functools

import jax
import jax.numpy as jnp
import numpy as np
from jax import lax
from jax.experimental import pallas as pl
from jax.experimental.pallas import tpu as pltpu
from jax.sharding import PartitionSpec as P

D = 8192
KV = 1024
L = 2
H = 512
HID = 32
NF = 6
AHEAD = 2
RB = 256
CB = 256
RQ = 8
UR = 4 * RQ
UT = RB // UR
NU = L * UT
SIZES = (1, 2, 2, 3, 3, 2, 2, 1)
NC = len(SIZES)
STARTS = tuple(sum(SIZES[:k]) for k in range(NC))
HALF = STARTS.index(UT)
ORDER = (
    (0, 0), (0, 1), (0, 2), (1, 0), (1, 1), (1, 2), (2, 0), (0, 3), (2, 1), (0, 4), (1, 3), (3, 1), (2, 2), (0, 5),
    (2, 3), (0, 6), (1, 4), (0, 7), (3, 0), ("p", 0), (3, 2), (4, 1), (3, 3), (1, 5), (4, 0), (1, 7), (4, 3), (4, 2),
    (1, 6), (2, 4), (5, 0), (2, 5), (5, 1), (5, 2), (5, 3), ("x", 0), (2, 6), (2, 7), ("a", 0), (3, 4), (3, 5),
    (3, 6), (3, 7), (4, 4), (4, 5), (4, 6), (4, 7), ("c", 0), (5, 4), (5, 5), (5, 6), (5, 7),
)
MESH = pl.DeviceIdType.MESH
F32 = jnp.float32
BF16 = jnp.bfloat16
DECAYS = tuple(np.float32(v) for v in (0.5, 0.9, 0.99))


def lane_to_rows(row):
    return jnp.transpose(jnp.broadcast_to(row, (128, 128)))


def rows_to_lane(block):
    return jnp.transpose(block)[0:1, :]


def twice(v):
    return jnp.concatenate([v, v], 1)


def network(begin, end, g_ref, m_refs, p_ref, row_ref, col_ref, norm_ref, wst_ref, w2_ref, mod_ref, out_ref):
    ones = jnp.where(lax.broadcasted_iota(jnp.int32, (16, CB), 0) < 2, 1.0, 0.0).astype(BF16)

    def tile(at):
        g = g_ref[at, :]
        p = p_ref[at, :]
        scale = lax.rsqrt(twice(row_ref[at, :]) * col_ref[...] + 1e-08)
        ins = [g * scale] + [m[at, :] * scale for m in m_refs]
        ins += [p * twice(norm_ref[0:1, :]), g * twice(norm_ref[1:2, :])]
        ins = jnp.concatenate(ins, 0)
        high = ins.astype(BF16)
        low = (ins - high.astype(F32)).astype(BF16)
        units = jnp.dot(
            wst_ref[:, 0:160], jnp.concatenate([high, low, high, ones], 0), preferred_element_type=F32
        )
        direction = jnp.zeros((8, CB), F32)
        magnitude = jnp.zeros((8, CB), F32)
        for h in range(HID):
            u = jnp.maximum(units[h * 8:(h + 1) * 8, :], 0.0)
            direction = direction + twice(w2_ref[0, h:h + 1, :]) * u
            magnitude = magnitude + twice(w2_ref[1, h:h + 1, :]) * u
        rate = twice(mod_ref[HID:HID + 1, :])
        gain = twice(mod_ref[HID + 1:HID + 2, :])
        out_ref[at, :] = p - rate * direction * jnp.exp(gain * magnitude)

    def step(i, carry):
        for u in range(8):
            tile(pl.ds(pl.multiple_of(i * 64 + u * 8, 8), 8))
        return carry

    lax.fori_loop(begin, end, step, 0)


def kernel(
    grads, params, moments, row_stat, col_stat, hidden, cell, input_w, recur_w, gate_bias, head_w, head_bias, w1, w2,
    n_params, n_moms, v_params, gsum, rowrep, colrow, norms, wst, w2rep, mod, n_rows, n_cols, n_hid, n_cell,
    graw, stage, acc, r1a, r1b, r2a, r2b,
    v_moms, v_row, v_col, v_hid, v_cell, v_iw, v_rw, v_gb, headt, v_hb, v_w1, v_w2,
    hidrep, colacc, macc, pacc, pre, hbcol, pa, cr, pb, zb, zr, pr, sr,
    in_sem, g_sem, s_sem, d_rs, r1a_rs, r1b_rs, r2a_rs, r2b_rs, c_ss, c_rs, z_ss, z_rs, p_ss, p_rs, o_ss, o_rs, met,
):
    dp = lax.axis_index("dp")
    z = lax.axis_index("tensor")
    x = dp // 8
    y = (dp // 2) % 4
    c = dp % 2

    def dev(dx=0, dy=0, dc=0, dz=0):
        return (((x + dx) % 4) * 8 + ((y + dy) % 4) * 2 + (c + dc) % 2, (z + dz) % 4)

    def send(src, dst, ss, rs, target):
        pltpu.make_async_remote_copy(
            src_ref=src, dst_ref=dst, send_sem=ss, recv_sem=rs, device_id=target, device_id_type=MESH
        ).start()

    def wait_all(ref, sem):
        pltpu.make_async_copy(ref, ref, sem).wait()

    def g_copy(k):
        l = STARTS[k] // UT
        part = pl.ds(STARTS[k] % UT * UR, SIZES[k] * UR)
        return pltpu.make_async_copy(
            grads.at[l, :, :, :, part, :], graw.at[l, :, :, :, part, :], g_sem.at[k]
        )

    for k in range(AHEAD):
        g_copy(k).start()
    barrier = pltpu.get_barrier_semaphore()

    near = (dev(dc=1), dev(dx=1), dev(dx=3), dev(dy=1), dev(dy=3), dev(dz=1), dev(dz=3))
    for target in near:
        pl.semaphore_signal(barrier, inc=1, device_id=target, device_id_type=MESH)

    ins = [
        pltpu.make_async_copy(a, b, in_sem.at[i])
        for i, (a, b) in enumerate(
            (
                (params, v_params), (moments, v_moms), (row_stat, v_row), (col_stat, v_col), (hidden, v_hid),
                (cell, v_cell), (input_w, v_iw), (recur_w, v_rw), (gate_bias, v_gb), (head_w, headt),
                (head_bias, v_hb), (w1, v_w1), (w2, v_w2),
            )
        )
    ]
    def load_more(k):
        if k + AHEAD < NC:
            g_copy(k + AHEAD).start()
        if k == 1:
            for copy in ins:
                copy.start()

    def units(k):
        return pl.ds(STARTS[k], SIZES[k])

    def spread(k, core, write):
        l = STARTS[k] // UT

        def step(i, carry):
            a, b = i // 4, i % 4
            for u in range(STARTS[k], STARTS[k] + SIZES[k]):
                v = graw[l, a, b, core, pl.ds(u % UT * UR, UR), :].astype(F32)
                for q in range(4):
                    write(u, q, a if q < 2 else b, b if q < 2 else a, v[q * RQ:(q + 1) * RQ, :])
            return carry

        lax.fori_loop(0, 16, step, 0)

    def stage_d(k):
        g_copy(k).wait()
        load_more(k)

        def write(u, q, i, j, v):
            stage[u, q, i, j] = v

        spread(k, 1 - c, write)
        if k == 0:
            pl.semaphore_wait(barrier, 7)
        send(stage.at[units(k)], acc.at[units(k)], s_sem.at[0], d_rs.at[k], dev(dc=1))

    first = (x, y)
    second = (y, x)
    ways = ((dev(dx=1), dev(dx=3)), (dev(dy=1), dev(dy=3)))

    def stage_1(k):
        wait_all(acc.at[units(k)], d_rs.at[k])

        def write(u, q, i, j, v):
            acc[u, q, i, j] += v

        spread(k, c, write)
        un = units(k)
        for h in range(2):
            i0, (plus, minus), qa, qb = first[h], ways[h], 2 * h, 2 * h + 1
            send(acc.at[un, qa, (i0 + 2) % 4], r1a.at[un, qa], s_sem.at[1], r1a_rs.at[k], plus)
            send(acc.at[un, qb, (i0 + 2) % 4], r1a.at[un, qb], s_sem.at[1], r1a_rs.at[k], minus)
        for h in range(2):
            i0, (plus, minus), qa, qb = first[h], ways[h], 2 * h, 2 * h + 1
            send(acc.at[un, qb, (i0 + 1) % 4], r1b.at[un, qb, 0], s_sem.at[2], r1b_rs.at[k], plus)
            send(acc.at[un, qa, (i0 + 3) % 4], r1b.at[un, qa, 1], s_sem.at[2], r1b_rs.at[k], minus)

    def stage_2(k):
        un = units(k)
        wait_all(r1a.at[un], r1a_rs.at[k])
        for h in range(2):
            i0, (plus, minus), qa, qb = first[h], ways[h], 2 * h, 2 * h + 1
            acc[un, qa, (i0 + 1) % 4] += r1a[un, qa]
            send(acc.at[un, qa, (i0 + 1) % 4], r1b.at[un, qa, 0], s_sem.at[2], r1b_rs.at[k], plus)
            acc[un, qb, (i0 + 3) % 4] += r1a[un, qb]
            send(acc.at[un, qb, (i0 + 3) % 4], r1b.at[un, qb, 1], s_sem.at[2], r1b_rs.at[k], minus)

    def stage_3(k):
        un = units(k)
        wait_all(r1b.at[un], r1b_rs.at[k])
        for h in range(2):
            i0, j0, (plus, minus), qa, qb = first[h], second[h], ways[1 - h], 2 * h, 2 * h + 1
            for q in (qa, qb):
                acc[un, q, i0] += r1b[un, q, 0] + r1b[un, q, 1]
            send(acc.at[un, qa, i0, (j0 + 2) % 4], r2a.at[un, qa], s_sem.at[3], r2a_rs.at[k], plus)
            send(acc.at[un, qb, i0, (j0 + 2) % 4], r2a.at[un, qb], s_sem.at[3], r2a_rs.at[k], minus)
            send(acc.at[un, qb, i0, (j0 + 1) % 4], r2b.at[un, qb, 0], s_sem.at[4], r2b_rs.at[k], plus)
            send(acc.at[un, qa, i0, (j0 + 3) % 4], r2b.at[un, qa, 1], s_sem.at[4], r2b_rs.at[k], minus)

    def stage_4(k):
        un = units(k)
        wait_all(r2a.at[un], r2a_rs.at[k])
        for h in range(2):
            i0, j0, (plus, minus), qa, qb = first[h], second[h], ways[1 - h], 2 * h, 2 * h + 1
            acc[un, qa, i0, (j0 + 1) % 4] += r2a[un, qa]
            send(acc.at[un, qa, i0, (j0 + 1) % 4], r2b.at[un, qa, 0], s_sem.at[4], r2b_rs.at[k], plus)
            acc[un, qb, i0, (j0 + 3) % 4] += r2a[un, qb]
            send(acc.at[un, qb, i0, (j0 + 3) % 4], r2b.at[un, qb, 1], s_sem.at[4], r2b_rs.at[k], minus)

    def stage_5(k):
        l = STARTS[k] // UT
        wait_all(r2b.at[units(k)], r2b_rs.at[k])
        for u in range(STARTS[k], STARTS[k] + SIZES[k]):
            for q in range(4):
                span = pl.ds(u % UT * UR + q * RQ, RQ)
                g = acc[u, q, first[q // 2], second[q // 2]] + r2b[u, q, 0] + r2b[u, q, 1]
                gsum[l, span, :] = g
                sq = g * g
                rowrep[l, span, :] = jnp.broadcast_to(jnp.sum(sq, 1, keepdims=True), (RQ, 128))
                colacc[l] += sq
                for n in range(3):
                    m = DECAYS[n] * v_moms[n, l, span, :] + (np.float32(1) - DECAYS[n]) * g
                    n_moms[n, l, span, :] = m
                    macc[l, n] += m * m

    lane = lax.broadcasted_iota(jnp.int32, (1, 128), 1)

    def prepare():
        for copy in ins:
            copy.wait()
        colacc[...] = jnp.zeros_like(colacc)
        macc[...] = jnp.zeros_like(macc)
        for l in range(L):
            def square(i, s):
                v = v_params[l, pl.ds(pl.multiple_of(i * 8, 8), 8), :]
                return s + v * v

            pacc[l] = lax.fori_loop(0, RB // 8, square, jnp.zeros((8, CB), F32))
        reps = [jnp.concatenate([lane_to_rows(v_hid[l:l + 1, i * 128:(i + 1) * 128]) for i in range(4)], 0) for l in range(L)]
        for l in range(L):
            hidrep[l] = reps[l]

        def recur(i, sums):
            at = pl.ds(pl.multiple_of(i * 8, 8), 8)
            w = v_rw[at, :]
            return tuple(sums[l] + w * jnp.tile(hidrep[l, at, :], (1, 16)) for l in range(L))

        sums = lax.fori_loop(0, H // 8, recur, tuple(jnp.zeros((8, 4 * H), F32) for _ in range(L)))
        for l in range(L):
            pre[l] = jnp.sum(sums[l], 0, keepdims=True) + v_gb[...]
        hbcol[...] = lane_to_rows(jnp.concatenate([v_hb[...], jnp.zeros((1, 126 - HID), F32)], 1))[0:HID + 2, :]
        w1t = jnp.concatenate([v_w1[...], jnp.zeros((128 - NF, HID), F32)], 0)
        w1t = jnp.transpose(jnp.concatenate([w1t, jnp.zeros((128, 128 - HID), F32)], 1))[0:HID, :]
        at = lax.broadcasted_iota(jnp.int32, (HID, 256), 1)
        wide = jnp.zeros((HID, 256), F32)
        for n in range(NF):
            hit = ((at // 8) % NF == n) & (at < 144)
            wide = jnp.where(hit, jnp.broadcast_to(w1t[:, n:n + 1], (HID, 256)), wide)
        tall = jnp.broadcast_to(wide[:, None, :], (HID, 8, 256)).reshape(HID * 8, 256)
        tall_at = lax.broadcasted_iota(jnp.int32, (HID * 8, 256), 1)
        tall_row = lax.broadcasted_iota(jnp.int32, (HID * 8, 256), 0)
        tall = jnp.where(tall_at % 8 == tall_row % 8, tall, 0.0)
        high = tall.astype(BF16).astype(F32)
        tall = jnp.where(tall_at < 96, high, tall - high).astype(BF16)
        for l in range(L):
            wst[l] = tall
        for o in range(2):
            row = jnp.concatenate([v_w2[o:o + 1, :], jnp.zeros((1, 128 - HID), F32)], 1)
            w2rep[o] = lane_to_rows(row)[0:HID, :]

    def total(v):
        return jnp.sum(jnp.sum(v, 0, keepdims=True), 1, keepdims=True)

    def put(values):
        row = jnp.zeros((1, 128), F32)
        for j, v in enumerate(values):
            row = jnp.where(lane == j, v, row)
        return row

    def pick(row, j):
        return jnp.sum(jnp.where(lane == j, row, 0.0), 1, keepdims=True)

    def exchange(l):
        sums = [colacc[l], macc[l, 0], macc[l, 1], macc[l, 2], pacc[l]]
        pa[l, :, 0:128] = put([total(v) for v in sums] + [jnp.sum(v_row[l:l + 1, :], 1, keepdims=True)])
        pa[l, :, 128:384] = jnp.sum(colacc[l], 0, keepdims=True)
        send(pa.at[l], cr.at[l], c_ss.at[l], c_rs.at[l], dev(dc=1))
        for i in range(2):
            zb[l, :, (i + 1) * 128:(i + 2) * 128] = rows_to_lane(rowrep[l, i * 128:(i + 1) * 128, :])

    def announce(l):
        wait_all(cr.at[l], c_rs.at[l])
        pb[l] = pa[l] + cr[l]
        zb[l, :, 0:128] = pb[l, :, 0:128]

        def other(i, carry):
            j = i % 15 + 1
            target = dev(j // 4, j % 4, 0, 1 + (1 + i // 15) % 3)
            send(pb.at[l, :, pl.ds(0, 128)], sr.at[l, i], o_ss.at[l], o_rs.at[l], target)
            return carry

        def plane(j, carry):
            send(pb.at[l], pr.at[l, j - 1], p_ss.at[l], p_rs.at[l], dev(j // 4, j % 4))
            return carry

        lax.fori_loop(0, 15, other, 0)
        lax.fori_loop(1, 16, plane, 0)
        lax.fori_loop(15, 45, other, 0)
        for dz in range(1, 4):
            send(zb.at[l], zr.at[l, dz - 1], z_ss.at[l], z_rs.at[l], dev(dz=dz))

    def control(l):
        wait_all(zr.at[l], z_rs.at[l])
        got = zb[l] + zr[l, 0] + zr[l, 1] + zr[l, 2]
        new = 0.9 * v_row[l:l + 1, :] + 0.1 * got[:, 128:384] / KV
        n_rows[l:l + 1, :] = new
        for i in range(2):
            rowrep[l, i * 128:(i + 1) * 128, :] = lane_to_rows(new[:, i * 128:(i + 1) * 128])
        wait_all(pr.at[l], p_rs.at[l])
        near = jnp.sum(pr[l], 0)
        new = 0.9 * v_col[l:l + 1, :] + 0.1 * (pb[l, :, 128:384] + near[:, 128:384]) / D
        n_cols[l:l + 1, :] = new
        wait_all(sr.at[l], o_rs.at[l])
        sums = got[:, 0:128] + near[:, 0:128] + jnp.sum(sr[l], 0)
        means = sums / (D * KV)
        stats = jnp.log(means + 1e-06)
        gates = pre[l]
        for j in range(5):
            gates = gates + pick(stats, j) * v_iw[j:j + 1, :]
        i_g = jax.nn.sigmoid(gates[:, 0:H])
        f_g = jax.nn.sigmoid(gates[:, H:2 * H])
        c_g = jnp.tanh(gates[:, 2 * H:3 * H])
        o_g = jax.nn.sigmoid(gates[:, 3 * H:])
        new_cell = f_g * v_cell[l:l + 1, :] + i_g * c_g
        new_hid = o_g * jnp.tanh(new_cell)
        n_cell[l:l + 1, :] = new_cell
        n_hid[l:l + 1, :] = new_hid
        m = jnp.sum(headt[...] * new_hid, 1, keepdims=True) + hbcol[...]
        mod[l, 0:HID + 2, :] = jnp.broadcast_to(m, (HID + 2, 128))
        mod[l, HID:HID + 1, :] = jnp.broadcast_to(jnp.exp(m[HID:HID + 1, :]), (1, 128))
        mod[l, HID + 1:HID + 2, :] = jnp.broadcast_to(0.5 * m[HID + 1:HID + 2, :], (1, 128))
        bias = jnp.broadcast_to(m[0:HID, None, :], (HID, 8, 128)).reshape(HID * 8, 128)
        high = bias.astype(BF16).astype(F32)
        side = wst[l, :, 128:256].astype(F32)
        side = jnp.where(lane == 16, high, jnp.where(lane == 17, bias - high, side))
        wst[l, :, 128:256] = side.astype(BF16)
        row_mean = (0.9 * (pick(sums, 5) / 4) + 0.1 * pick(sums, 0) / KV) / D
        colrow[l] = new / row_mean
        norms[l, 0:1, :] = jnp.broadcast_to(lax.rsqrt(pick(means, 4) + 1e-06), (1, 128))
        norms[l, 1:2, :] = jnp.broadcast_to(lax.rsqrt(pick(means, 0) + 1e-06), (1, 128))

    def network_0(begin, end):
        network(
            begin, end, gsum.at[0], [n_moms.at[n, 0] for n in range(3)], v_params.at[0], rowrep.at[0], colrow.at[0],
            norms.at[0], wst.at[0], w2rep, mod.at[0], n_params,
        )

    def meet(n):
        for target in (dev(dz=1), dev(dz=3)):
            pl.semaphore_signal(met.at[n], inc=1, device_id=target, device_id_type=MESH)

    steps = (stage_d, stage_1, stage_2, stage_3, stage_4, stage_5)
    for step, k in ORDER:
        if step == "p":
            prepare()
        elif step == "x":
            exchange(0)
        elif step == "a":
            pl.semaphore_wait(met.at[1], 2)
            announce(0)
        elif step == "c":
            control(0)
        else:
            steps[step](k)
        if step == 5 and k == 0:
            meet(0)
        if step == 5 and k == 1:
            pl.semaphore_wait(met.at[0], 2)
            meet(1)
    exchange(1)
    announce(1)
    network_0(0, 4)
    control(1)
    wait_all(acc, s_sem.at[0])
    wait_all(r1a, s_sem.at[1])
    wait_all(r1b, s_sem.at[2])
    wait_all(r2a, s_sem.at[3])
    wait_all(r2b, s_sem.at[4])
    for l in range(L):
        wait_all(cr.at[l], c_ss.at[l])
        wait_all(zr.at[l], z_ss.at[l])
        wait_all(pr.at[l], p_ss.at[l])
        wait_all(sr.at[l], o_ss.at[l])


def finish(
    params_0, moms, params, gsum, rowrep, colrow, norms, wst, w2rep, mod, rows, cols, hid, cell,
    o_params, o_moms, o_rows, o_cols, o_hid, o_cell, params_1, sem,
):
    copies = [
        pltpu.make_async_copy(a, b, sem.at[i])
        for i, (a, b) in enumerate(
            ((moms, o_moms), (params_0, o_params.at[0]), (rows, o_rows), (cols, o_cols), (hid, o_hid), (cell, o_cell))
        )
    ]
    for copy in copies:
        copy.start()
    for part in range(2):
        network(
            2 * part, 2 * part + 2, gsum.at[1], [moms.at[n, 1] for n in range(3)], params.at[1], rowrep.at[1],
            colrow.at[1], norms.at[1], wst.at[1], w2rep, mod.at[1], params_1,
        )
        half = pl.ds(part * RB // 2, RB // 2)
        copy = pltpu.make_async_copy(params_1.at[half, :], o_params.at[1, half, :], sem.at[6 + part])
        copy.start()
        copies.append(copy)
    for copy in copies:
        copy.wait()


def body(grads, params, moments, row_stat, col_stat, hidden, cell, input_w, recur_w, gate_bias, head_w, head_bias, w1, w2):
    hbm = pl.BlockSpec(memory_space=pltpu.HBM)
    held = pl.BlockSpec(memory_space=pltpu.VMEM)
    vmem = pltpu.VMEM
    dma = pltpu.SemaphoreType.DMA
    quarter = (RQ, CB)
    between = (
        vmem((RB, CB), F32),
        vmem((3, L, RB, CB), F32),
        vmem((L, RB, CB), F32),
        vmem((L, RB, CB), F32),
        vmem((L, RB, 128), F32),
        vmem((L, 1, CB), F32),
        vmem((L, 2, 128), F32),
        vmem((L, HID * 8, 256), BF16),
        vmem((2, HID, 128), F32),
        vmem((L, HID + 2, 128), F32),
        vmem((L, RB), F32),
        vmem((L, CB), F32),
        vmem((L, H), F32),
        vmem((L, H), F32),
    )
    operands = (
        grads.reshape(L, 4, 4, 2, RB, CB), params, moments, row_stat, col_stat, hidden, cell, input_w, recur_w,
        gate_bias.reshape(1, 4 * H), head_w.T, head_bias.reshape(1, HID + 2), w1, w2.T,
    )
    results = pl.pallas_call(
        kernel,
        out_shape=between,
        in_specs=[hbm] * 14,
        out_specs=(held,) * len(between),
        scratch_shapes=[
            vmem((L, 4, 4, 2, RB, CB), BF16),
            vmem((NU, 4, 4, 4) + quarter, F32),
            vmem((NU, 4, 4, 4) + quarter, F32),
            vmem((NU, 4, 4) + quarter, F32),
            vmem((NU, 4, 2, 4) + quarter, F32),
            vmem((NU, 4) + quarter, F32),
            vmem((NU, 4, 2) + quarter, F32),
            vmem((3, L, RB, CB), F32),
            vmem((L, RB), F32),
            vmem((L, CB), F32),
            vmem((L, H), F32),
            vmem((L, H), F32),
            vmem((5, 4 * H), F32),
            vmem((H, 4 * H), F32),
            vmem((1, 4 * H), F32),
            vmem((HID + 2, H), F32),
            vmem((1, HID + 2), F32),
            vmem((NF, HID), F32),
            vmem((2, HID), F32),
            vmem((L, H, 128), F32),
            vmem((L, 8, CB), F32),
            vmem((L, 3, 8, CB), F32),
            vmem((L, 8, CB), F32),
            vmem((L, 1, 4 * H), F32),
            vmem((HID + 2, 128), F32),
            vmem((L, 1, 384), F32),
            vmem((L, 1, 384), F32),
            vmem((L, 1, 384), F32),
            vmem((L, 1, 384), F32),
            vmem((L, 3, 1, 384), F32),
            vmem((L, 15, 1, 384), F32),
            vmem((L, 45, 1, 128), F32),
            dma((13,)),
            dma((NC,)),
            dma((5,)),
        ]
        + [dma((NC,))] * 5
        + [dma((L,))] * 8
        + [pltpu.SemaphoreType.REGULAR((2,))],
        compiler_params=pltpu.CompilerParams(
            collective_id=0, has_side_effects=True, vmem_limit_bytes=46 * 2**20
        ),
        name="update",
    )(*[pltpu.with_memory_space_constraint(v, pltpu.HBM) for v in operands])
    return pl.pallas_call(
        finish,
        out_shape=(
            jax.ShapeDtypeStruct((L, RB, CB), F32),
            jax.ShapeDtypeStruct((3, L, RB, CB), F32),
            jax.ShapeDtypeStruct((L, RB), F32),
            jax.ShapeDtypeStruct((L, CB), F32),
            jax.ShapeDtypeStruct((L, H), F32),
            jax.ShapeDtypeStruct((L, H), F32),
        ),
        in_specs=[held] * len(between),
        out_specs=(hbm,) * 6,
        scratch_shapes=[vmem((RB, CB), F32), dma((8,))],
        compiler_params=pltpu.CompilerParams(vmem_limit_bytes=16 * 2**20),
        name="finish",
    )(*results)


def solution(mesh):
    return jax.shard_map(
        body,
        mesh=mesh,
        in_specs=(
            P("dp", None, None, "tensor"),
            P(None, "dp", "tensor"),
            P(None, None, "dp", "tensor"),
            P(None, "dp"),
            P(None, "tensor"),
        )
        + (P(),) * 9,
        out_specs=(
            P(None, "dp", "tensor"),
            P(None, None, "dp", "tensor"),
            P(None, "dp"),
            P(None, "tensor"),
            P(),
            P(),
        ),
        check_vma=False,
    )
```

```python
import functools

import jax
import jax.numpy as jnp
import numpy as np
from jax import lax
from jax.experimental import pallas as pl
from jax.experimental.pallas import tpu as pltpu
from jax.sharding import PartitionSpec as P

D = 8192
KV = 1024
L = 2
H = 512
HID = 32
NF = 6
AHEAD = 2
RB = 256
CB = 256
RQ = 8
UR = 4 * RQ
UT = RB // UR
NU = L * UT
SIZES = (1, 2, 2, 3, 3, 3, 2)
NC = len(SIZES)
STARTS = tuple(sum(SIZES[:k]) for k in range(NC))
HALF = STARTS.index(UT)
DIRECT_1 = NC
DIRECT_2 = NC - 2
ORDER = (
    (0, 0), (0, 1), (1, 0), (1, 1), (0, 2), (0, 3), (2, 0), (1, 2), (1, 3), (2, 1), (3, 0), (0, 4), (2, 2), ("p", 0),
    ("p", 1), (0, 5), (2, 3), (1, 4), ("p", 2), (4, 0), (3, 2), (3, 3), (3, 1), (1, 5), ("p", 3), (0, 6), (4, 1),
    (5, 0), (2, 4), (4, 2), (4, 3), (1, 6), (5, 1), (2, 5), (5, 2), (5, 3), ("x", 0), (2, 6), (3, 4), ("a", 0),
    (3, 5), (4, 4), (3, 6), ("c", 0), (4, 6), (5, 4), (4, 5), (5, 5), (5, 6),
)
MESH = pl.DeviceIdType.MESH
F32 = jnp.float32
BF16 = jnp.bfloat16
DECAYS = tuple(np.float32(v) for v in (0.5, 0.9, 0.99))


def lane_to_rows(row):
    return jnp.transpose(jnp.broadcast_to(row, (128, 128)))


def rows_to_lane(block):
    return jnp.transpose(block)[0:1, :]


def twice(v):
    return jnp.concatenate([v, v], 1)


def network(begin, end, g_ref, m_refs, p_ref, row_ref, col_ref, norm_ref, wst_ref, w2_ref, mod_ref, out_ref):
    ones = jnp.where(lax.broadcasted_iota(jnp.int32, (16, CB), 0) < 2, 1.0, 0.0).astype(BF16)

    def tile(at):
        g = g_ref[at, :]
        p = p_ref[at, :]
        scale = lax.rsqrt(twice(row_ref[at, :]) * col_ref[...] + 1e-08)
        ins = [g * scale] + [m[at, :] * scale for m in m_refs]
        ins += [p * twice(norm_ref[0:1, :]), g * twice(norm_ref[1:2, :])]
        ins = jnp.concatenate(ins, 0)
        high = ins.astype(BF16)
        low = (ins - high.astype(F32)).astype(BF16)
        units = jnp.dot(
            wst_ref[:, 0:160], jnp.concatenate([high, low, high, ones], 0), preferred_element_type=F32
        )
        direction = jnp.zeros((8, CB), F32)
        magnitude = jnp.zeros((8, CB), F32)
        for h in range(HID):
            u = jnp.maximum(units[h * 8:(h + 1) * 8, :], 0.0)
            direction = direction + twice(w2_ref[0, h:h + 1, :]) * u
            magnitude = magnitude + twice(w2_ref[1, h:h + 1, :]) * u
        rate = twice(mod_ref[HID:HID + 1, :])
        gain = twice(mod_ref[HID + 1:HID + 2, :])
        out_ref[at, :] = p - rate * direction * jnp.exp(gain * magnitude)

    def step(i, carry):
        for u in range(8):
            tile(pl.ds(pl.multiple_of(i * 64 + u * 8, 8), 8))
        return carry

    lax.fori_loop(begin, end, step, 0)


def kernel(
    grads, params, moments, row_stat, col_stat, hidden, cell, input_w, recur_w, gate_bias, head_w, head_bias, w1, w2,
    n_params, n_moms, v_params, gsum, rowrep, colrow, norms, wst, w2rep, mod, n_rows, n_cols, n_hid, n_cell,
    graw, stage, acc, r1a, r1b, r2a, r2b,
    v_moms, v_row, v_col, v_hid, v_cell, v_iw, v_rw, v_gb, headt, v_hb, v_w1, v_w2,
    hidrep, recsum, colacc, macc, pacc, pre, hbcol, pa, cr, pb, zb, zr, pr, sr,
    in_sem, g_sem, s_sem, d_rs, r1a_rs, r1b_rs, r2a_rs, r2b_rs, c_ss, c_rs, z_ss, z_rs, p_ss, p_rs, o_ss, o_rs, met,
):
    dp = lax.axis_index("dp")
    z = lax.axis_index("tensor")
    x = dp // 8
    y = (dp // 2) % 4
    c = dp % 2

    def dev(dx=0, dy=0, dc=0, dz=0):
        return (((x + dx) % 4) * 8 + ((y + dy) % 4) * 2 + (c + dc) % 2, (z + dz) % 4)

    def send(src, dst, ss, rs, target):
        pltpu.make_async_remote_copy(
            src_ref=src, dst_ref=dst, send_sem=ss, recv_sem=rs, device_id=target, device_id_type=MESH
        ).start()

    def wait_all(ref, sem):
        pltpu.make_async_copy(ref, ref, sem).wait()

    def g_copy(k):
        l = STARTS[k] // UT
        part = pl.ds(STARTS[k] % UT * UR, SIZES[k] * UR)
        return pltpu.make_async_copy(
            grads.at[l, :, :, :, part, :], graw.at[l, :, :, :, part, :], g_sem.at[k]
        )

    for k in range(AHEAD):
        g_copy(k).start()
    barrier = pltpu.get_barrier_semaphore()

    near = (dev(dc=1), dev(dx=1), dev(dx=3), dev(dy=1), dev(dy=3), dev(dz=1), dev(dz=3))
    for target in near:
        pl.semaphore_signal(barrier, inc=1, device_id=target, device_id_type=MESH)

    ins = [
        pltpu.make_async_copy(a, b, in_sem.at[i])
        for i, (a, b) in enumerate(
            (
                (params, v_params), (moments, v_moms), (row_stat, v_row), (col_stat, v_col), (hidden, v_hid),
                (cell, v_cell), (input_w, v_iw), (recur_w, v_rw), (gate_bias, v_gb), (head_w, headt),
                (head_bias, v_hb), (w1, v_w1), (w2, v_w2),
            )
        )
    ]
    def load_more(k):
        if k + AHEAD < NC:
            g_copy(k + AHEAD).start()
        if k == 1:
            for copy in ins:
                copy.start()

    def units(k):
        return pl.ds(STARTS[k], SIZES[k])

    def spread(k, core, write):
        l = STARTS[k] // UT

        def step(i, carry):
            a, b = i // 4, i % 4
            for u in range(STARTS[k], STARTS[k] + SIZES[k]):
                v = graw[l, a, b, core, pl.ds(u % UT * UR, UR), :].astype(F32)
                for q in range(4):
                    write(u, q, a if q < 2 else b, b if q < 2 else a, v[q * RQ:(q + 1) * RQ, :])
            return carry

        lax.fori_loop(0, 16, step, 0)

    def stage_d(k):
        g_copy(k).wait()
        load_more(k)

        def write(u, q, i, j, v):
            stage[u, q, i, j] = v

        spread(k, 1 - c, write)
        if k == 0:
            pl.semaphore_wait(barrier, 7)
        send(stage.at[units(k)], acc.at[units(k)], s_sem.at[0], d_rs.at[k], dev(dc=1))

    first = (x, y)
    second = (y, x)
    ways = ((dev(dx=1), dev(dx=3)), (dev(dy=1), dev(dy=3)))
    across = (dev(dx=2), dev(dy=2))

    def stage_1(k):
        wait_all(acc.at[units(k)], d_rs.at[k])

        def write(u, q, i, j, v):
            acc[u, q, i, j] += v

        spread(k, c, write)
        un = units(k)
        if k >= DIRECT_1:
            for h in range(2):
                i0, (plus, minus), both = first[h], ways[h], pl.ds(2 * h, 2)
                send(acc.at[un, both, (i0 + 2) % 4], r1a.at[un, both], s_sem.at[1], r1a_rs.at[k], across[h])
                send(acc.at[un, both, (i0 + 1) % 4], r1b.at[un, both, 0], s_sem.at[2], r1b_rs.at[k], plus)
                send(acc.at[un, both, (i0 + 3) % 4], r1b.at[un, both, 1], s_sem.at[2], r1b_rs.at[k], minus)
            return
        for h in range(2):
            i0, (plus, minus), qa, qb = first[h], ways[h], 2 * h, 2 * h + 1
            send(acc.at[un, qa, (i0 + 2) % 4], r1a.at[un, qa], s_sem.at[1], r1a_rs.at[k], plus)
            send(acc.at[un, qb, (i0 + 2) % 4], r1a.at[un, qb], s_sem.at[1], r1a_rs.at[k], minus)
        for h in range(2):
            i0, (plus, minus), qa, qb = first[h], ways[h], 2 * h, 2 * h + 1
            send(acc.at[un, qb, (i0 + 1) % 4], r1b.at[un, qb, 0], s_sem.at[2], r1b_rs.at[k], plus)
            send(acc.at[un, qa, (i0 + 3) % 4], r1b.at[un, qa, 1], s_sem.at[2], r1b_rs.at[k], minus)

    def stage_2(k):
        if k >= DIRECT_1:
            return
        un = units(k)
        wait_all(r1a.at[un], r1a_rs.at[k])
        for h in range(2):
            i0, (plus, minus), qa, qb = first[h], ways[h], 2 * h, 2 * h + 1
            acc[un, qa, (i0 + 1) % 4] += r1a[un, qa]
            send(acc.at[un, qa, (i0 + 1) % 4], r1b.at[un, qa, 0], s_sem.at[2], r1b_rs.at[k], plus)
            acc[un, qb, (i0 + 3) % 4] += r1a[un, qb]
            send(acc.at[un, qb, (i0 + 3) % 4], r1b.at[un, qb, 1], s_sem.at[2], r1b_rs.at[k], minus)

    def stage_3(k):
        un = units(k)
        wait_all(r1b.at[un], r1b_rs.at[k])
        if k >= DIRECT_1:
            wait_all(r1a.at[un], r1a_rs.at[k])
        for h in range(2):
            i0, j0, (plus, minus), qa, qb = first[h], second[h], ways[1 - h], 2 * h, 2 * h + 1
            for q in (qa, qb):
                got = r1b[un, q, 0] + r1b[un, q, 1]
                if k >= DIRECT_1:
                    got = got + r1a[un, q]
                acc[un, q, i0] += got
            if k >= DIRECT_2:
                both = pl.ds(2 * h, 2)
                send(acc.at[un, both, i0, (j0 + 2) % 4], r2a.at[un, both], s_sem.at[3], r2a_rs.at[k], across[1 - h])
                send(acc.at[un, both, i0, (j0 + 1) % 4], r2b.at[un, both, 0], s_sem.at[4], r2b_rs.at[k], plus)
                send(acc.at[un, both, i0, (j0 + 3) % 4], r2b.at[un, both, 1], s_sem.at[4], r2b_rs.at[k], minus)
                continue
            send(acc.at[un, qa, i0, (j0 + 2) % 4], r2a.at[un, qa], s_sem.at[3], r2a_rs.at[k], plus)
            send(acc.at[un, qb, i0, (j0 + 2) % 4], r2a.at[un, qb], s_sem.at[3], r2a_rs.at[k], minus)
            send(acc.at[un, qb, i0, (j0 + 1) % 4], r2b.at[un, qb, 0], s_sem.at[4], r2b_rs.at[k], plus)
            send(acc.at[un, qa, i0, (j0 + 3) % 4], r2b.at[un, qa, 1], s_sem.at[4], r2b_rs.at[k], minus)

    def stage_4(k):
        if k >= DIRECT_2:
            return
        un = units(k)
        wait_all(r2a.at[un], r2a_rs.at[k])
        for h in range(2):
            i0, j0, (plus, minus), qa, qb = first[h], second[h], ways[1 - h], 2 * h, 2 * h + 1
            acc[un, qa, i0, (j0 + 1) % 4] += r2a[un, qa]
            send(acc.at[un, qa, i0, (j0 + 1) % 4], r2b.at[un, qa, 0], s_sem.at[4], r2b_rs.at[k], plus)
            acc[un, qb, i0, (j0 + 3) % 4] += r2a[un, qb]
            send(acc.at[un, qb, i0, (j0 + 3) % 4], r2b.at[un, qb, 1], s_sem.at[4], r2b_rs.at[k], minus)

    def stage_5(k):
        l = STARTS[k] // UT
        wait_all(r2b.at[units(k)], r2b_rs.at[k])
        if k >= DIRECT_2:
            wait_all(r2a.at[units(k)], r2a_rs.at[k])
        for u in range(STARTS[k], STARTS[k] + SIZES[k]):
            for q in range(4):
                span = pl.ds(u % UT * UR + q * RQ, RQ)
                g = acc[u, q, first[q // 2], second[q // 2]] + r2b[u, q, 0] + r2b[u, q, 1]
                if k >= DIRECT_2:
                    g = g + r2a[u, q]
                gsum[l, span, :] = g
                sq = g * g
                rowrep[l, span, :] = jnp.broadcast_to(jnp.sum(sq, 1, keepdims=True), (RQ, 128))
                colacc[l] += sq
                for n in range(3):
                    m = DECAYS[n] * v_moms[n, l, span, :] + (np.float32(1) - DECAYS[n]) * g
                    n_moms[n, l, span, :] = m
                    macc[l, n] += m * m

    lane = lax.broadcasted_iota(jnp.int32, (1, 128), 1)

    def prepare_0():
        for copy in ins:
            copy.wait()
        colacc[...] = jnp.zeros_like(colacc)
        macc[...] = jnp.zeros_like(macc)
        for l in range(L):
            def square(i, s):
                v = v_params[l, pl.ds(pl.multiple_of(i * 8, 8), 8), :]
                return s + v * v

            pacc[l] = lax.fori_loop(0, RB // 8, square, jnp.zeros((8, CB), F32))
        recsum[...] = jnp.zeros_like(recsum)
        reps = [jnp.concatenate([lane_to_rows(v_hid[l:l + 1, i * 128:(i + 1) * 128]) for i in range(4)], 0) for l in range(L)]
        for l in range(L):
            hidrep[l] = reps[l]

    def recurrent(begin, end):
        def recur(i, sums):
            at = pl.ds(pl.multiple_of(i * 8, 8), 8)
            w = v_rw[at, :]
            return tuple(sums[l] + w * jnp.tile(hidrep[l, at, :], (1, 16)) for l in range(L))

        sums = lax.fori_loop(begin, end, recur, tuple(recsum[l] for l in range(L)))
        for l in range(L):
            recsum[l] = sums[l]

    def prepare_1():
        recurrent(0, H // 16)

    def prepare_2():
        recurrent(H // 16, H // 8)
        for l in range(L):
            pre[l] = jnp.sum(recsum[l], 0, keepdims=True) + v_gb[...]

    def prepare_3():
        hbcol[...] = lane_to_rows(jnp.concatenate([v_hb[...], jnp.zeros((1, 126 - HID), F32)], 1))[0:HID + 2, :]
        w1t = jnp.concatenate([v_w1[...], jnp.zeros((128 - NF, HID), F32)], 0)
        w1t = jnp.transpose(jnp.concatenate([w1t, jnp.zeros((128, 128 - HID), F32)], 1))[0:HID, :]
        at = lax.broadcasted_iota(jnp.int32, (HID, 256), 1)
        wide = jnp.zeros((HID, 256), F32)
        for n in range(NF):
            hit = ((at // 8) % NF == n) & (at < 144)
            wide = jnp.where(hit, jnp.broadcast_to(w1t[:, n:n + 1], (HID, 256)), wide)
        tall = jnp.broadcast_to(wide[:, None, :], (HID, 8, 256)).reshape(HID * 8, 256)
        tall_at = lax.broadcasted_iota(jnp.int32, (HID * 8, 256), 1)
        tall_row = lax.broadcasted_iota(jnp.int32, (HID * 8, 256), 0)
        tall = jnp.where(tall_at % 8 == tall_row % 8, tall, 0.0)
        high = tall.astype(BF16).astype(F32)
        tall = jnp.where(tall_at < 96, high, tall - high).astype(BF16)
        for l in range(L):
            wst[l] = tall
        for o in range(2):
            row = jnp.concatenate([v_w2[o:o + 1, :], jnp.zeros((1, 128 - HID), F32)], 1)
            w2rep[o] = lane_to_rows(row)[0:HID, :]

    def total(v):
        return jnp.sum(jnp.sum(v, 0, keepdims=True), 1, keepdims=True)

    def put(values):
        row = jnp.zeros((1, 128), F32)
        for j, v in enumerate(values):
            row = jnp.where(lane == j, v, row)
        return row

    def pick(row, j):
        return jnp.sum(jnp.where(lane == j, row, 0.0), 1, keepdims=True)

    def exchange(l):
        sums = [colacc[l], macc[l, 0], macc[l, 1], macc[l, 2], pacc[l]]
        pa[l, :, 0:128] = put([total(v) for v in sums] + [jnp.sum(v_row[l:l + 1, :], 1, keepdims=True)])
        pa[l, :, 128:384] = jnp.sum(colacc[l], 0, keepdims=True)
        send(pa.at[l], cr.at[l], c_ss.at[l], c_rs.at[l], dev(dc=1))
        for i in range(2):
            zb[l, :, (i + 1) * 128:(i + 2) * 128] = rows_to_lane(rowrep[l, i * 128:(i + 1) * 128, :])

    def announce(l):
        wait_all(cr.at[l], c_rs.at[l])
        pb[l] = pa[l] + cr[l]
        zb[l, :, 0:128] = pb[l, :, 0:128]

        def other(i, carry):
            j = i % 15 + 1
            target = dev(j // 4, j % 4, 0, 1 + (1 + i // 15) % 3)
            send(pb.at[l, :, pl.ds(0, 128)], sr.at[l, i], o_ss.at[l], o_rs.at[l], target)
            return carry

        def plane(j, carry):
            send(pb.at[l], pr.at[l, j - 1], p_ss.at[l], p_rs.at[l], dev(j // 4, j % 4))
            return carry

        lax.fori_loop(0, 15, other, 0)
        lax.fori_loop(1, 16, plane, 0)
        lax.fori_loop(15, 45, other, 0)
        for dz in range(1, 4):
            send(zb.at[l], zr.at[l, dz - 1], z_ss.at[l], z_rs.at[l], dev(dz=dz))

    def control(l):
        wait_all(zr.at[l], z_rs.at[l])
        got = zb[l] + zr[l, 0] + zr[l, 1] + zr[l, 2]
        new = 0.9 * v_row[l:l + 1, :] + 0.1 * got[:, 128:384] / KV
        n_rows[l:l + 1, :] = new
        for i in range(2):
            rowrep[l, i * 128:(i + 1) * 128, :] = lane_to_rows(new[:, i * 128:(i + 1) * 128])
        wait_all(pr.at[l], p_rs.at[l])
        near = jnp.sum(pr[l], 0)
        new = 0.9 * v_col[l:l + 1, :] + 0.1 * (pb[l, :, 128:384] + near[:, 128:384]) / D
        n_cols[l:l + 1, :] = new
        wait_all(sr.at[l], o_rs.at[l])
        sums = got[:, 0:128] + near[:, 0:128] + jnp.sum(sr[l], 0)
        means = sums / (D * KV)
        stats = jnp.log(means + 1e-06)
        gates = pre[l]
        for j in range(5):
            gates = gates + pick(stats, j) * v_iw[j:j + 1, :]
        i_g = jax.nn.sigmoid(gates[:, 0:H])
        f_g = jax.nn.sigmoid(gates[:, H:2 * H])
        c_g = jnp.tanh(gates[:, 2 * H:3 * H])
        o_g = jax.nn.sigmoid(gates[:, 3 * H:])
        new_cell = f_g * v_cell[l:l + 1, :] + i_g * c_g
        new_hid = o_g * jnp.tanh(new_cell)
        n_cell[l:l + 1, :] = new_cell
        n_hid[l:l + 1, :] = new_hid
        m = jnp.sum(headt[...] * new_hid, 1, keepdims=True) + hbcol[...]
        mod[l, 0:HID + 2, :] = jnp.broadcast_to(m, (HID + 2, 128))
        mod[l, HID:HID + 1, :] = jnp.broadcast_to(jnp.exp(m[HID:HID + 1, :]), (1, 128))
        mod[l, HID + 1:HID + 2, :] = jnp.broadcast_to(0.5 * m[HID + 1:HID + 2, :], (1, 128))
        bias = jnp.broadcast_to(m[0:HID, None, :], (HID, 8, 128)).reshape(HID * 8, 128)
        high = bias.astype(BF16).astype(F32)
        side = wst[l, :, 128:256].astype(F32)
        side = jnp.where(lane == 16, high, jnp.where(lane == 17, bias - high, side))
        wst[l, :, 128:256] = side.astype(BF16)
        row_mean = (0.9 * (pick(sums, 5) / 4) + 0.1 * pick(sums, 0) / KV) / D
        colrow[l] = new / row_mean
        norms[l, 0:1, :] = jnp.broadcast_to(lax.rsqrt(pick(means, 4) + 1e-06), (1, 128))
        norms[l, 1:2, :] = jnp.broadcast_to(lax.rsqrt(pick(means, 0) + 1e-06), (1, 128))

    def network_0(begin, end):
        network(
            begin, end, gsum.at[0], [n_moms.at[n, 0] for n in range(3)], v_params.at[0], rowrep.at[0], colrow.at[0],
            norms.at[0], wst.at[0], w2rep, mod.at[0], n_params,
        )

    def meet(n):
        for target in (dev(dz=1), dev(dz=3)):
            pl.semaphore_signal(met.at[n], inc=1, device_id=target, device_id_type=MESH)

    steps = (stage_d, stage_1, stage_2, stage_3, stage_4, stage_5)
    for step, k in ORDER:
        if step == "p":
            (prepare_0, prepare_1, prepare_2, prepare_3)[k]()
        elif step == "x":
            exchange(0)
        elif step == "a":
            pl.semaphore_wait(met.at[1], 2)
            announce(0)
        elif step == "c":
            control(0)
        else:
            steps[step](k)
        if step == 5 and k == 0:
            meet(0)
        if step == 5 and k == 1:
            pl.semaphore_wait(met.at[0], 2)
            meet(1)
    exchange(1)
    announce(1)
    network_0(0, 4)
    wait_all(acc, s_sem.at[0])
    wait_all(r1a, s_sem.at[1])
    wait_all(r1b, s_sem.at[2])
    wait_all(r2a, s_sem.at[3])
    wait_all(r2b, s_sem.at[4])
    control(1)
    for l in range(L):
        wait_all(cr.at[l], c_ss.at[l])
        wait_all(zr.at[l], z_ss.at[l])
        wait_all(pr.at[l], p_ss.at[l])
        wait_all(sr.at[l], o_ss.at[l])


def finish(
    params_0, moms, params, gsum, rowrep, colrow, norms, wst, w2rep, mod, rows, cols, hid, cell,
    o_params, o_moms, o_rows, o_cols, o_hid, o_cell, params_1, sem,
):
    copies = [
        pltpu.make_async_copy(a, b, sem.at[i])
        for i, (a, b) in enumerate(
            ((moms, o_moms), (params_0, o_params.at[0]), (rows, o_rows), (cols, o_cols), (hid, o_hid), (cell, o_cell))
        )
    ]
    for copy in copies:
        copy.start()
    for part in range(2):
        network(
            2 * part, 2 * part + 2, gsum.at[1], [moms.at[n, 1] for n in range(3)], params.at[1], rowrep.at[1],
            colrow.at[1], norms.at[1], wst.at[1], w2rep, mod.at[1], params_1,
        )
        half = pl.ds(part * RB // 2, RB // 2)
        copy = pltpu.make_async_copy(params_1.at[half, :], o_params.at[1, half, :], sem.at[6 + part])
        copy.start()
        copies.append(copy)
    for copy in copies:
        copy.wait()


def body(grads, params, moments, row_stat, col_stat, hidden, cell, input_w, recur_w, gate_bias, head_w, head_bias, w1, w2):
    hbm = pl.BlockSpec(memory_space=pltpu.HBM)
    held = pl.BlockSpec(memory_space=pltpu.VMEM)
    vmem = pltpu.VMEM
    dma = pltpu.SemaphoreType.DMA
    quarter = (RQ, CB)
    between = (
        vmem((RB, CB), F32),
        vmem((3, L, RB, CB), F32),
        vmem((L, RB, CB), F32),
        vmem((L, RB, CB), F32),
        vmem((L, RB, 128), F32),
        vmem((L, 1, CB), F32),
        vmem((L, 2, 128), F32),
        vmem((L, HID * 8, 256), BF16),
        vmem((2, HID, 128), F32),
        vmem((L, HID + 2, 128), F32),
        vmem((L, RB), F32),
        vmem((L, CB), F32),
        vmem((L, H), F32),
        vmem((L, H), F32),
    )
    operands = (
        grads.reshape(L, 4, 4, 2, RB, CB), params, moments, row_stat, col_stat, hidden, cell, input_w, recur_w,
        gate_bias.reshape(1, 4 * H), head_w.T, head_bias.reshape(1, HID + 2), w1, w2.T,
    )
    results = pl.pallas_call(
        kernel,
        out_shape=between,
        in_specs=[hbm] * 14,
        out_specs=(held,) * len(between),
        scratch_shapes=[
            vmem((L, 4, 4, 2, RB, CB), BF16),
            vmem((NU, 4, 4, 4) + quarter, F32),
            vmem((NU, 4, 4, 4) + quarter, F32),
            vmem((NU, 4, 4) + quarter, F32),
            vmem((NU, 4, 2, 4) + quarter, F32),
            vmem((NU, 4) + quarter, F32),
            vmem((NU, 4, 2) + quarter, F32),
            vmem((3, L, RB, CB), F32),
            vmem((L, RB), F32),
            vmem((L, CB), F32),
            vmem((L, H), F32),
            vmem((L, H), F32),
            vmem((5, 4 * H), F32),
            vmem((H, 4 * H), F32),
            vmem((1, 4 * H), F32),
            vmem((HID + 2, H), F32),
            vmem((1, HID + 2), F32),
            vmem((NF, HID), F32),
            vmem((2, HID), F32),
            vmem((L, H, 128), F32),
            vmem((L, 8, 4 * H), F32),
            vmem((L, 8, CB), F32),
            vmem((L, 3, 8, CB), F32),
            vmem((L, 8, CB), F32),
            vmem((L, 1, 4 * H), F32),
            vmem((HID + 2, 128), F32),
            vmem((L, 1, 384), F32),
            vmem((L, 1, 384), F32),
            vmem((L, 1, 384), F32),
            vmem((L, 1, 384), F32),
            vmem((L, 3, 1, 384), F32),
            vmem((L, 15, 1, 384), F32),
            vmem((L, 45, 1, 128), F32),
            dma((13,)),
            dma((NC,)),
            dma((5,)),
        ]
        + [dma((NC,))] * 5
        + [dma((L,))] * 8
        + [pltpu.SemaphoreType.REGULAR((2,))],
        compiler_params=pltpu.CompilerParams(
            collective_id=0, has_side_effects=True, vmem_limit_bytes=46 * 2**20
        ),
        name="update",
    )(*[pltpu.with_memory_space_constraint(v, pltpu.HBM) for v in operands])
    return pl.pallas_call(
        finish,
        out_shape=(
            jax.ShapeDtypeStruct((L, RB, CB), F32),
            jax.ShapeDtypeStruct((3, L, RB, CB), F32),
            jax.ShapeDtypeStruct((L, RB), F32),
            jax.ShapeDtypeStruct((L, CB), F32),
            jax.ShapeDtypeStruct((L, H), F32),
            jax.ShapeDtypeStruct((L, H), F32),
        ),
        in_specs=[held] * len(between),
        out_specs=(hbm,) * 6,
        scratch_shapes=[vmem((RB, CB), F32), dma((8,))],
        compiler_params=pltpu.CompilerParams(vmem_limit_bytes=16 * 2**20),
        name="finish",
    )(*results)


def solution(mesh):
    return jax.shard_map(
        body,
        mesh=mesh,
        in_specs=(
            P("dp", None, None, "tensor"),
            P(None, "dp", "tensor"),
            P(None, None, "dp", "tensor"),
            P(None, "dp"),
            P(None, "tensor"),
        )
        + (P(),) * 9,
        out_specs=(
            P(None, "dp", "tensor"),
            P(None, None, "dp", "tensor"),
            P(None, "dp"),
            P(None, "tensor"),
            P(),
            P(),
        ),
        check_vma=False,
    )
```

```python
import functools

import jax
import jax.numpy as jnp
import numpy as np
from jax import lax
from jax.experimental import pallas as pl
from jax.experimental.pallas import tpu as pltpu
from jax.sharding import PartitionSpec as P

D = 8192
KV = 1024
L = 2
H = 512
HID = 32
NF = 6
AHEAD = 2
RB = 256
CB = 256
RQ = 8
UR = 4 * RQ
UT = RB // UR
NU = L * UT
SIZES = (1, 2, 2, 3, 3, 3, 2)
NC = len(SIZES)
STARTS = tuple(sum(SIZES[:k]) for k in range(NC))
HALF = STARTS.index(UT)
DIRECT_1 = NC
DIRECT_2 = NC - 2
ORDER = (
    (0, 0), (0, 1), (1, 0), (1, 1), (0, 2), (0, 3), (2, 0), (1, 2), (1, 3), (2, 1), (3, 0), (0, 4), (2, 2), ("p", 0),
    ("p", 1), (0, 5), (2, 3), (1, 4), ("p", 2), (4, 0), (3, 2), (3, 3), (3, 1), (1, 5), ("p", 3), (0, 6), (4, 1),
    (5, 0), (2, 4), (4, 2), (4, 3), (1, 6), (5, 1), (2, 5), (5, 2), (5, 3), ("x", 0), (2, 6), (3, 4), ("a", 0),
    (3, 5), (4, 4), (3, 6), ("c", 0), (4, 6), (5, 4), (4, 5), (5, 5), (5, 6),
)
MESH = pl.DeviceIdType.MESH
F32 = jnp.float32
BF16 = jnp.bfloat16
DECAYS = tuple(np.float32(v) for v in (0.5, 0.9, 0.99))


def lane_to_rows(row):
    return jnp.transpose(jnp.broadcast_to(row, (128, 128)))


def rows_to_lane(block):
    return jnp.transpose(block)[0:1, :]


def twice(v):
    return jnp.concatenate([v, v], 1)


def network(begin, end, g_ref, m_refs, p_ref, row_ref, col_ref, norm_ref, wst_ref, w2_ref, mod_ref, out_ref):
    ones = jnp.where(lax.broadcasted_iota(jnp.int32, (16, CB), 0) < 2, 1.0, 0.0).astype(BF16)

    def tile(at):
        g = g_ref[at, :]
        p = p_ref[at, :]
        scale = lax.rsqrt(twice(row_ref[at, :]) * col_ref[...] + 1e-08)
        ins = [g * scale] + [m[at, :] * scale for m in m_refs]
        ins += [p * twice(norm_ref[0:1, :]), g * twice(norm_ref[1:2, :])]
        ins = jnp.concatenate(ins, 0)
        high = ins.astype(BF16)
        low = (ins - high.astype(F32)).astype(BF16)
        units = jnp.dot(
            wst_ref[:, 0:160], jnp.concatenate([high, low, high, ones], 0), preferred_element_type=F32
        )
        direction = jnp.zeros((8, CB), F32)
        magnitude = jnp.zeros((8, CB), F32)
        for h in range(HID):
            u = jnp.maximum(units[h * 8:(h + 1) * 8, :], 0.0)
            direction = direction + twice(w2_ref[0, h:h + 1, :]) * u
            magnitude = magnitude + twice(w2_ref[1, h:h + 1, :]) * u
        rate = twice(mod_ref[HID:HID + 1, :])
        gain = twice(mod_ref[HID + 1:HID + 2, :])
        out_ref[at, :] = p - rate * direction * jnp.exp(gain * magnitude)

    def step(i, carry):
        for u in range(8):
            tile(pl.ds(pl.multiple_of(i * 64 + u * 8, 8), 8))
        return carry

    lax.fori_loop(begin, end, step, 0)


def kernel(
    grads, params, moments, row_stat, col_stat, hidden, cell, input_w, recur_w, gate_bias, head_w, head_bias, w1, w2,
    n_params, n_moms, v_params, gsum, rowrep, colrow, norms, wst, w2rep, mod, n_rows, n_cols, n_hid, n_cell,
    graw, stage, acc, r1a, r1b, r2a, r2b,
    v_moms, v_row, v_col, v_hid, v_cell, v_iw, v_rw, v_gb, headt, v_hb, v_w1, v_w2,
    hidrep, recsum, colacc, macc, pacc, pre, hbcol, pa, cr, pb, zb, zr, pr, sr,
    in_sem, g_sem, s_sem, d_rs, r1a_rs, r1b_rs, r2a_rs, r2b_rs, c_ss, c_rs, z_ss, z_rs, p_ss, p_rs, o_ss, o_rs, met,
):
    dp = lax.axis_index("dp")
    z = lax.axis_index("tensor")
    x = dp // 8
    y = (dp // 2) % 4
    c = dp % 2

    at_x = [(x + d) % 4 * 8 for d in range(4)]
    at_y = [(y + d) % 4 * 2 for d in range(4)]
    at_c = [c, 1 - c]
    at_z = [(z + d) % 4 for d in range(4)]

    def dev(dx=0, dy=0, dc=0, dz=0):
        return (at_x[dx] + at_y[dy] + at_c[dc], at_z[dz])

    def send(src, dst, ss, rs, target):
        pltpu.make_async_remote_copy(
            src_ref=src, dst_ref=dst, send_sem=ss, recv_sem=rs, device_id=target, device_id_type=MESH
        ).start()

    def wait_all(ref, sem):
        pltpu.make_async_copy(ref, ref, sem).wait()

    def g_copy(k):
        l = STARTS[k] // UT
        part = pl.ds(STARTS[k] % UT * UR, SIZES[k] * UR)
        return pltpu.make_async_copy(
            grads.at[l, :, :, :, part, :], graw.at[l, :, :, :, part, :], g_sem.at[k]
        )

    for k in range(AHEAD):
        g_copy(k).start()
    barrier = pltpu.get_barrier_semaphore()

    near = (dev(dc=1), dev(dx=1), dev(dx=3), dev(dy=1), dev(dy=3), dev(dz=1), dev(dz=3))
    for target in near:
        pl.semaphore_signal(barrier, inc=1, device_id=target, device_id_type=MESH)

    ins = [
        pltpu.make_async_copy(a, b, in_sem.at[i])
        for i, (a, b) in enumerate(
            (
                (params, v_params), (moments, v_moms), (row_stat, v_row), (col_stat, v_col), (hidden, v_hid),
                (cell, v_cell), (input_w, v_iw), (recur_w, v_rw), (gate_bias, v_gb), (head_w, headt),
                (head_bias, v_hb), (w1, v_w1), (w2, v_w2),
            )
        )
    ]
    def load_more(k):
        if k + AHEAD < NC:
            g_copy(k + AHEAD).start()
        if k == 1:
            for copy in ins:
                copy.start()

    def units(k):
        return pl.ds(STARTS[k], SIZES[k])

    def spread(k, core, write):
        l = STARTS[k] // UT

        def step(i, carry):
            a, b = i // 4, i % 4
            for u in range(STARTS[k], STARTS[k] + SIZES[k]):
                v = graw[l, a, b, core, pl.ds(u % UT * UR, UR), :].astype(F32)
                for q in range(4):
                    write(u, q, a if q < 2 else b, b if q < 2 else a, v[q * RQ:(q + 1) * RQ, :])
            return carry

        lax.fori_loop(0, 16, step, 0)

    def stage_d(k):
        g_copy(k).wait()
        load_more(k)

        def write(u, q, i, j, v):
            stage[u, q, i, j] = v

        spread(k, 1 - c, write)
        if k == 0:
            pl.semaphore_wait(barrier, 7)
        send(stage.at[units(k)], acc.at[units(k)], s_sem.at[0], d_rs.at[k], dev(dc=1))

    first = (x, y)
    second = (y, x)
    ways = ((dev(dx=1), dev(dx=3)), (dev(dy=1), dev(dy=3)))
    across = (dev(dx=2), dev(dy=2))

    def stage_1(k):
        wait_all(acc.at[units(k)], d_rs.at[k])

        def write(u, q, i, j, v):
            acc[u, q, i, j] += v

        spread(k, c, write)
        un = units(k)
        if k >= DIRECT_1:
            for h in range(2):
                i0, (plus, minus), both = first[h], ways[h], pl.ds(2 * h, 2)
                send(acc.at[un, both, (i0 + 2) % 4], r1a.at[un, both], s_sem.at[1], r1a_rs.at[k], across[h])
                send(acc.at[un, both, (i0 + 1) % 4], r1b.at[un, both, 0], s_sem.at[2], r1b_rs.at[k], plus)
                send(acc.at[un, both, (i0 + 3) % 4], r1b.at[un, both, 1], s_sem.at[2], r1b_rs.at[k], minus)
            return
        for h in range(2):
            i0, (plus, minus), qa, qb = first[h], ways[h], 2 * h, 2 * h + 1
            send(acc.at[un, qa, (i0 + 2) % 4], r1a.at[un, qa], s_sem.at[1], r1a_rs.at[k], plus)
            send(acc.at[un, qb, (i0 + 2) % 4], r1a.at[un, qb], s_sem.at[1], r1a_rs.at[k], minus)
        for h in range(2):
            i0, (plus, minus), qa, qb = first[h], ways[h], 2 * h, 2 * h + 1
            send(acc.at[un, qb, (i0 + 1) % 4], r1b.at[un, qb, 0], s_sem.at[2], r1b_rs.at[k], plus)
            send(acc.at[un, qa, (i0 + 3) % 4], r1b.at[un, qa, 1], s_sem.at[2], r1b_rs.at[k], minus)

    def stage_2(k):
        if k >= DIRECT_1:
            return
        un = units(k)
        wait_all(r1a.at[un], r1a_rs.at[k])
        for h in range(2):
            i0, (plus, minus), qa, qb = first[h], ways[h], 2 * h, 2 * h + 1
            acc[un, qa, (i0 + 1) % 4] += r1a[un, qa]
            send(acc.at[un, qa, (i0 + 1) % 4], r1b.at[un, qa, 0], s_sem.at[2], r1b_rs.at[k], plus)
            acc[un, qb, (i0 + 3) % 4] += r1a[un, qb]
            send(acc.at[un, qb, (i0 + 3) % 4], r1b.at[un, qb, 1], s_sem.at[2], r1b_rs.at[k], minus)

    def stage_3(k):
        un = units(k)
        wait_all(r1b.at[un], r1b_rs.at[k])
        if k >= DIRECT_1:
            wait_all(r1a.at[un], r1a_rs.at[k])
        for h in range(2):
            i0, j0, (plus, minus), qa, qb = first[h], second[h], ways[1 - h], 2 * h, 2 * h + 1
            for q in (qa, qb):
                got = r1b[un, q, 0] + r1b[un, q, 1]
                if k >= DIRECT_1:
                    got = got + r1a[un, q]
                acc[un, q, i0] += got
            if k >= DIRECT_2:
                both = pl.ds(2 * h, 2)
                send(acc.at[un, both, i0, (j0 + 2) % 4], r2a.at[un, both], s_sem.at[3], r2a_rs.at[k], across[1 - h])
                send(acc.at[un, both, i0, (j0 + 1) % 4], r2b.at[un, both, 0], s_sem.at[4], r2b_rs.at[k], plus)
                send(acc.at[un, both, i0, (j0 + 3) % 4], r2b.at[un, both, 1], s_sem.at[4], r2b_rs.at[k], minus)
                continue
            send(acc.at[un, qa, i0, (j0 + 2) % 4], r2a.at[un, qa], s_sem.at[3], r2a_rs.at[k], plus)
            send(acc.at[un, qb, i0, (j0 + 2) % 4], r2a.at[un, qb], s_sem.at[3], r2a_rs.at[k], minus)
            send(acc.at[un, qb, i0, (j0 + 1) % 4], r2b.at[un, qb, 0], s_sem.at[4], r2b_rs.at[k], plus)
            send(acc.at[un, qa, i0, (j0 + 3) % 4], r2b.at[un, qa, 1], s_sem.at[4], r2b_rs.at[k], minus)

    def stage_4(k):
        if k >= DIRECT_2:
            return
        un = units(k)
        wait_all(r2a.at[un], r2a_rs.at[k])
        for h in range(2):
            i0, j0, (plus, minus), qa, qb = first[h], second[h], ways[1 - h], 2 * h, 2 * h + 1
            acc[un, qa, i0, (j0 + 1) % 4] += r2a[un, qa]
            send(acc.at[un, qa, i0, (j0 + 1) % 4], r2b.at[un, qa, 0], s_sem.at[4], r2b_rs.at[k], plus)
            acc[un, qb, i0, (j0 + 3) % 4] += r2a[un, qb]
            send(acc.at[un, qb, i0, (j0 + 3) % 4], r2b.at[un, qb, 1], s_sem.at[4], r2b_rs.at[k], minus)

    def stage_5(k):
        l = STARTS[k] // UT
        wait_all(r2b.at[units(k)], r2b_rs.at[k])
        if k >= DIRECT_2:
            wait_all(r2a.at[units(k)], r2a_rs.at[k])
        for u in range(STARTS[k], STARTS[k] + SIZES[k]):
            for q in range(4):
                span = pl.ds(u % UT * UR + q * RQ, RQ)
                g = acc[u, q, first[q // 2], second[q // 2]] + r2b[u, q, 0] + r2b[u, q, 1]
                if k >= DIRECT_2:
                    g = g + r2a[u, q]
                gsum[l, span, :] = g
                sq = g * g
                rowrep[l, span, :] = jnp.broadcast_to(jnp.sum(sq, 1, keepdims=True), (RQ, 128))
                colacc[l] += sq
                for n in range(3):
                    m = DECAYS[n] * v_moms[n, l, span, :] + (np.float32(1) - DECAYS[n]) * g
                    n_moms[n, l, span, :] = m
                    macc[l, n] += m * m

    lane = lax.broadcasted_iota(jnp.int32, (1, 128), 1)

    def prepare_0():
        for copy in ins:
            copy.wait()
        colacc[...] = jnp.zeros_like(colacc)
        macc[...] = jnp.zeros_like(macc)
        for l in range(L):
            def square(i, s):
                v = v_params[l, pl.ds(pl.multiple_of(i * 8, 8), 8), :]
                return s + v * v

            pacc[l] = lax.fori_loop(0, RB // 8, square, jnp.zeros((8, CB), F32))
        recsum[...] = jnp.zeros_like(recsum)
        reps = [jnp.concatenate([lane_to_rows(v_hid[l:l + 1, i * 128:(i + 1) * 128]) for i in range(4)], 0) for l in range(L)]
        for l in range(L):
            hidrep[l] = reps[l]

    def recurrent(begin, end):
        def recur(i, sums):
            at = pl.ds(pl.multiple_of(i * 8, 8), 8)
            w = v_rw[at, :]
            return tuple(sums[l] + w * jnp.tile(hidrep[l, at, :], (1, 16)) for l in range(L))

        sums = lax.fori_loop(begin, end, recur, tuple(recsum[l] for l in range(L)))
        for l in range(L):
            recsum[l] = sums[l]

    def prepare_1():
        recurrent(0, H // 16)

    def prepare_2():
        recurrent(H // 16, H // 8)
        for l in range(L):
            pre[l] = jnp.sum(recsum[l], 0, keepdims=True) + v_gb[...]

    def prepare_3():
        hbcol[...] = lane_to_rows(jnp.concatenate([v_hb[...], jnp.zeros((1, 126 - HID), F32)], 1))[0:HID + 2, :]
        w1t = jnp.concatenate([v_w1[...], jnp.zeros((128 - NF, HID), F32)], 0)
        w1t = jnp.transpose(jnp.concatenate([w1t, jnp.zeros((128, 128 - HID), F32)], 1))[0:HID, :]
        at = lax.broadcasted_iota(jnp.int32, (HID, 256), 1)
        wide = jnp.zeros((HID, 256), F32)
        for n in range(NF):
            hit = ((at // 8) % NF == n) & (at < 144)
            wide = jnp.where(hit, jnp.broadcast_to(w1t[:, n:n + 1], (HID, 256)), wide)
        tall = jnp.broadcast_to(wide[:, None, :], (HID, 8, 256)).reshape(HID * 8, 256)
        tall_at = lax.broadcasted_iota(jnp.int32, (HID * 8, 256), 1)
        tall_row = lax.broadcasted_iota(jnp.int32, (HID * 8, 256), 0)
        tall = jnp.where(tall_at % 8 == tall_row % 8, tall, 0.0)
        high = tall.astype(BF16).astype(F32)
        tall = jnp.where(tall_at < 96, high, tall - high).astype(BF16)
        for l in range(L):
            wst[l] = tall
        for o in range(2):
            row = jnp.concatenate([v_w2[o:o + 1, :], jnp.zeros((1, 128 - HID), F32)], 1)
            w2rep[o] = lane_to_rows(row)[0:HID, :]

    def total(v):
        return jnp.sum(jnp.sum(v, 0, keepdims=True), 1, keepdims=True)

    def put(values):
        row = jnp.zeros((1, 128), F32)
        for j, v in enumerate(values):
            row = jnp.where(lane == j, v, row)
        return row

    def pick(row, j):
        return jnp.sum(jnp.where(lane == j, row, 0.0), 1, keepdims=True)

    def exchange(l):
        sums = [colacc[l], macc[l, 0], macc[l, 1], macc[l, 2], pacc[l]]
        pa[l, :, 0:128] = put([total(v) for v in sums] + [jnp.sum(v_row[l:l + 1, :], 1, keepdims=True)])
        pa[l, :, 128:384] = jnp.sum(colacc[l], 0, keepdims=True)
        send(pa.at[l], cr.at[l], c_ss.at[l], c_rs.at[l], dev(dc=1))
        for i in range(2):
            zb[l, :, (i + 1) * 128:(i + 2) * 128] = rows_to_lane(rowrep[l, i * 128:(i + 1) * 128, :])

    def announce(l):
        wait_all(cr.at[l], c_rs.at[l])
        pb[l] = pa[l] + cr[l]
        zb[l, :, 0:128] = pb[l, :, 0:128]

        def others(n, dz):
            for j in range(1, 16):
                send(
                    pb.at[l, :, pl.ds(0, 128)], sr.at[l, 15 * n + j - 1], o_ss.at[l], o_rs.at[l], dev(j // 4, j % 4, 0, dz)
                )

        others(0, 2)
        for j in range(1, 16):
            send(pb.at[l], pr.at[l, j - 1], p_ss.at[l], p_rs.at[l], dev(j // 4, j % 4))
        others(1, 3)
        others(2, 1)
        for dz in range(1, 4):
            send(zb.at[l], zr.at[l, dz - 1], z_ss.at[l], z_rs.at[l], dev(dz=dz))

    def control(l):
        wait_all(zr.at[l], z_rs.at[l])
        got = zb[l] + zr[l, 0] + zr[l, 1] + zr[l, 2]
        new = 0.9 * v_row[l:l + 1, :] + 0.1 * got[:, 128:384] / KV
        n_rows[l:l + 1, :] = new
        for i in range(2):
            rowrep[l, i * 128:(i + 1) * 128, :] = lane_to_rows(new[:, i * 128:(i + 1) * 128])
        wait_all(pr.at[l], p_rs.at[l])
        near = jnp.sum(pr[l], 0)
        new = 0.9 * v_col[l:l + 1, :] + 0.1 * (pb[l, :, 128:384] + near[:, 128:384]) / D
        n_cols[l:l + 1, :] = new
        wait_all(sr.at[l], o_rs.at[l])
        sums = got[:, 0:128] + near[:, 0:128] + jnp.sum(sr[l], 0)
        means = sums / (D * KV)
        stats = jnp.log(means + 1e-06)
        gates = pre[l]
        for j in range(5):
            gates = gates + pick(stats, j) * v_iw[j:j + 1, :]
        i_g = jax.nn.sigmoid(gates[:, 0:H])
        f_g = jax.nn.sigmoid(gates[:, H:2 * H])
        c_g = jnp.tanh(gates[:, 2 * H:3 * H])
        o_g = jax.nn.sigmoid(gates[:, 3 * H:])
        new_cell = f_g * v_cell[l:l + 1, :] + i_g * c_g
        new_hid = o_g * jnp.tanh(new_cell)
        n_cell[l:l + 1, :] = new_cell
        n_hid[l:l + 1, :] = new_hid
        m = jnp.sum(headt[...] * new_hid, 1, keepdims=True) + hbcol[...]
        mod[l, 0:HID + 2, :] = jnp.broadcast_to(m, (HID + 2, 128))
        mod[l, HID:HID + 1, :] = jnp.broadcast_to(jnp.exp(m[HID:HID + 1, :]), (1, 128))
        mod[l, HID + 1:HID + 2, :] = jnp.broadcast_to(0.5 * m[HID + 1:HID + 2, :], (1, 128))
        bias = jnp.broadcast_to(m[0:HID, None, :], (HID, 8, 128)).reshape(HID * 8, 128)
        high = bias.astype(BF16).astype(F32)
        side = wst[l, :, 128:256].astype(F32)
        side = jnp.where(lane == 16, high, jnp.where(lane == 17, bias - high, side))
        wst[l, :, 128:256] = side.astype(BF16)
        row_mean = (0.9 * (pick(sums, 5) / 4) + 0.1 * pick(sums, 0) / KV) / D
        colrow[l] = new / row_mean
        norms[l, 0:1, :] = jnp.broadcast_to(lax.rsqrt(pick(means, 4) + 1e-06), (1, 128))
        norms[l, 1:2, :] = jnp.broadcast_to(lax.rsqrt(pick(means, 0) + 1e-06), (1, 128))

    def network_0(begin, end):
        network(
            begin, end, gsum.at[0], [n_moms.at[n, 0] for n in range(3)], v_params.at[0], rowrep.at[0], colrow.at[0],
            norms.at[0], wst.at[0], w2rep, mod.at[0], n_params,
        )

    def meet(n):
        for target in (dev(dz=1), dev(dz=3)):
            pl.semaphore_signal(met.at[n], inc=1, device_id=target, device_id_type=MESH)

    steps = (stage_d, stage_1, stage_2, stage_3, stage_4, stage_5)
    for step, k in ORDER:
        if step == "p":
            (prepare_0, prepare_1, prepare_2, prepare_3)[k]()
        elif step == "x":
            exchange(0)
        elif step == "a":
            pl.semaphore_wait(met.at[1], 2)
            announce(0)
        elif step == "c":
            control(0)
        else:
            steps[step](k)
        if step == 5 and k == 0:
            meet(0)
        if step == 5 and k == 1:
            pl.semaphore_wait(met.at[0], 2)
            meet(1)
    exchange(1)
    announce(1)
    network_0(0, 4)
    wait_all(acc, s_sem.at[0])
    wait_all(r1a, s_sem.at[1])
    wait_all(r1b, s_sem.at[2])
    wait_all(r2a, s_sem.at[3])
    wait_all(r2b, s_sem.at[4])
    control(1)
    for l in range(L):
        wait_all(cr.at[l], c_ss.at[l])
        wait_all(zr.at[l], z_ss.at[l])
        wait_all(pr.at[l], p_ss.at[l])
        wait_all(sr.at[l], o_ss.at[l])


def finish(
    params_0, moms, params, gsum, rowrep, colrow, norms, wst, w2rep, mod, rows, cols, hid, cell,
    o_params, o_moms, o_rows, o_cols, o_hid, o_cell, params_1, sem,
):
    copies = [
        pltpu.make_async_copy(a, b, sem.at[i])
        for i, (a, b) in enumerate(
            ((moms, o_moms), (params_0, o_params.at[0]), (rows, o_rows), (cols, o_cols), (hid, o_hid), (cell, o_cell))
        )
    ]
    for copy in copies:
        copy.start()
    for part in range(2):
        network(
            2 * part, 2 * part + 2, gsum.at[1], [moms.at[n, 1] for n in range(3)], params.at[1], rowrep.at[1],
            colrow.at[1], norms.at[1], wst.at[1], w2rep, mod.at[1], params_1,
        )
        half = pl.ds(part * RB // 2, RB // 2)
        copy = pltpu.make_async_copy(params_1.at[half, :], o_params.at[1, half, :], sem.at[6 + part])
        copy.start()
        copies.append(copy)
    for copy in copies:
        copy.wait()


def body(grads, params, moments, row_stat, col_stat, hidden, cell, input_w, recur_w, gate_bias, head_w, head_bias, w1, w2):
    hbm = pl.BlockSpec(memory_space=pltpu.HBM)
    held = pl.BlockSpec(memory_space=pltpu.VMEM)
    vmem = pltpu.VMEM
    dma = pltpu.SemaphoreType.DMA
    quarter = (RQ, CB)
    between = (
        vmem((RB, CB), F32),
        vmem((3, L, RB, CB), F32),
        vmem((L, RB, CB), F32),
        vmem((L, RB, CB), F32),
        vmem((L, RB, 128), F32),
        vmem((L, 1, CB), F32),
        vmem((L, 2, 128), F32),
        vmem((L, HID * 8, 256), BF16),
        vmem((2, HID, 128), F32),
        vmem((L, HID + 2, 128), F32),
        vmem((L, RB), F32),
        vmem((L, CB), F32),
        vmem((L, H), F32),
        vmem((L, H), F32),
    )
    operands = (
        grads.reshape(L, 4, 4, 2, RB, CB), params, moments, row_stat, col_stat, hidden, cell, input_w, recur_w,
        gate_bias.reshape(1, 4 * H), head_w.T, head_bias.reshape(1, HID + 2), w1, w2.T,
    )
    results = pl.pallas_call(
        kernel,
        out_shape=between,
        in_specs=[hbm] * 14,
        out_specs=(held,) * len(between),
        scratch_shapes=[
            vmem((L, 4, 4, 2, RB, CB), BF16),
            vmem((NU, 4, 4, 4) + quarter, F32),
            vmem((NU, 4, 4, 4) + quarter, F32),
            vmem((NU, 4, 4) + quarter, F32),
            vmem((NU, 4, 2, 4) + quarter, F32),
            vmem((NU, 4) + quarter, F32),
            vmem((NU, 4, 2) + quarter, F32),
            vmem((3, L, RB, CB), F32),
            vmem((L, RB), F32),
            vmem((L, CB), F32),
            vmem((L, H), F32),
            vmem((L, H), F32),
            vmem((5, 4 * H), F32),
            vmem((H, 4 * H), F32),
            vmem((1, 4 * H), F32),
            vmem((HID + 2, H), F32),
            vmem((1, HID + 2), F32),
            vmem((NF, HID), F32),
            vmem((2, HID), F32),
            vmem((L, H, 128), F32),
            vmem((L, 8, 4 * H), F32),
            vmem((L, 8, CB), F32),
            vmem((L, 3, 8, CB), F32),
            vmem((L, 8, CB), F32),
            vmem((L, 1, 4 * H), F32),
            vmem((HID + 2, 128), F32),
            vmem((L, 1, 384), F32),
            vmem((L, 1, 384), F32),
            vmem((L, 1, 384), F32),
            vmem((L, 1, 384), F32),
            vmem((L, 3, 1, 384), F32),
            vmem((L, 15, 1, 384), F32),
            vmem((L, 45, 1, 128), F32),
            dma((13,)),
            dma((NC,)),
            dma((5,)),
        ]
        + [dma((NC,))] * 5
        + [dma((L,))] * 8
        + [pltpu.SemaphoreType.REGULAR((2,))],
        compiler_params=pltpu.CompilerParams(
            collective_id=0, has_side_effects=True, vmem_limit_bytes=46 * 2**20
        ),
        name="update",
    )(*[pltpu.with_memory_space_constraint(v, pltpu.HBM) for v in operands])
    return pl.pallas_call(
        finish,
        out_shape=(
            jax.ShapeDtypeStruct((L, RB, CB), F32),
            jax.ShapeDtypeStruct((3, L, RB, CB), F32),
            jax.ShapeDtypeStruct((L, RB), F32),
            jax.ShapeDtypeStruct((L, CB), F32),
            jax.ShapeDtypeStruct((L, H), F32),
            jax.ShapeDtypeStruct((L, H), F32),
        ),
        in_specs=[held] * len(between),
        out_specs=(hbm,) * 6,
        scratch_shapes=[vmem((RB, CB), F32), dma((8,))],
        compiler_params=pltpu.CompilerParams(vmem_limit_bytes=16 * 2**20),
        name="finish",
    )(*results)


def solution(mesh):
    return jax.shard_map(
        body,
        mesh=mesh,
        in_specs=(
            P("dp", None, None, "tensor"),
            P(None, "dp", "tensor"),
            P(None, None, "dp", "tensor"),
            P(None, "dp"),
            P(None, "tensor"),
        )
        + (P(),) * 9,
        out_specs=(
            P(None, "dp", "tensor"),
            P(None, None, "dp", "tensor"),
            P(None, "dp"),
            P(None, "tensor"),
            P(),
            P(),
        ),
        check_vma=False,
    )
```

```python
import functools

import jax
import jax.numpy as jnp
import numpy as np
from jax import lax
from jax.experimental import pallas as pl
from jax.experimental.pallas import tpu as pltpu
from jax.sharding import PartitionSpec as P

D = 8192
KV = 1024
L = 2
H = 512
HID = 32
NF = 6
AHEAD = 2
RB = 256
CB = 256
RQ = 8
UR = 4 * RQ
UT = RB // UR
NU = L * UT
SIZES = (1, 2, 2, 3, 3, 3, 2)
NC = len(SIZES)
STARTS = tuple(sum(SIZES[:k]) for k in range(NC))
HALF = STARTS.index(UT)
DIRECT_1 = NC
DIRECT_2 = NC - 2
ORDER = (
    (0, 0), (0, 1), (1, 0), (1, 1), (0, 2), (0, 3), (2, 0), (1, 2), (1, 3), (2, 1), (3, 0), (0, 4), (2, 2), ("p", 0),
    ("p", 1), (0, 5), (2, 3), (1, 4), ("p", 2), (4, 0), (3, 2), (3, 3), (3, 1), (1, 5), ("p", 3), (0, 6), (4, 1),
    (5, 0), (2, 4), (4, 2), (4, 3), (1, 6), (5, 1), (2, 5), (5, 2), (5, 3), ("x", 0), (2, 6), (3, 4), ("a", 0),
    (3, 5), (4, 4), (3, 6), ("c", 0), (4, 6), (5, 4), (4, 5), (5, 5), (5, 6),
)
MESH = pl.DeviceIdType.MESH
F32 = jnp.float32
BF16 = jnp.bfloat16
DECAYS = tuple(np.float32(v) for v in (0.5, 0.9, 0.99))


def lane_to_rows(row):
    return jnp.transpose(jnp.broadcast_to(row, (128, 128)))


def rows_to_lane(block):
    return jnp.transpose(block)[0:1, :]


def twice(v):
    return jnp.concatenate([v, v], 1)


def network(begin, end, g_ref, m_refs, p_ref, row_ref, col_ref, norm_ref, wst_ref, w2_ref, mod_ref, out_ref):
    ones = jnp.where(lax.broadcasted_iota(jnp.int32, (16, CB), 0) < 2, 1.0, 0.0).astype(BF16)

    def tile(at):
        g = g_ref[at, :]
        p = p_ref[at, :]
        scale = lax.rsqrt(twice(row_ref[at, :]) * col_ref[...] + 1e-08)
        ins = [g * scale] + [m[at, :] * scale for m in m_refs]
        ins += [p * twice(norm_ref[0:1, :]), g * twice(norm_ref[1:2, :])]
        ins = jnp.concatenate(ins, 0)
        high = ins.astype(BF16)
        low = (ins - high.astype(F32)).astype(BF16)
        units = jnp.dot(
            wst_ref[:, 0:160], jnp.concatenate([high, low, high, ones], 0), preferred_element_type=F32
        )
        direction = jnp.zeros((8, CB), F32)
        magnitude = jnp.zeros((8, CB), F32)
        for h in range(HID):
            u = jnp.maximum(units[h * 8:(h + 1) * 8, :], 0.0)
            direction = direction + twice(w2_ref[0, h:h + 1, :]) * u
            magnitude = magnitude + twice(w2_ref[1, h:h + 1, :]) * u
        rate = twice(mod_ref[HID:HID + 1, :])
        gain = twice(mod_ref[HID + 1:HID + 2, :])
        out_ref[at, :] = p - rate * direction * jnp.exp(gain * magnitude)

    def step(i, carry):
        for u in range(8):
            tile(pl.ds(pl.multiple_of(i * 64 + u * 8, 8), 8))
        return carry

    lax.fori_loop(begin, end, step, 0)


def kernel(
    grads, params, moments, row_stat, col_stat, hidden, cell, input_w, recur_w, gate_bias, head_w, head_bias, w1, w2,
    n_params, n_moms, v_params, gsum, rowrep, colrow, norms, wst, w2rep, mod, n_rows, n_cols, n_hid, n_cell,
    graw, stage, acc, r1a, r1b, r2a, r2b,
    v_moms, v_row, v_col, v_hid, v_cell, v_iw, v_rw, v_gb, headt, v_hb, v_w1, v_w2,
    hidrep, recsum, colacc, macc, early, pre, hbcol, pa, cr, pb, zb, zr, pr, sr,
    in_sem, g_sem, s_sem, d_rs, r1a_rs, r1b_rs, r2a_rs, r2b_rs, c_ss, c_rs, z_ss, z_rs, p_ss, p_rs, o_ss, o_rs, met,
):
    dp = lax.axis_index("dp")
    z = lax.axis_index("tensor")
    x = dp // 8
    y = (dp // 2) % 4
    c = dp % 2

    at_x = [(x + d) % 4 * 8 for d in range(4)]
    at_y = [(y + d) % 4 * 2 for d in range(4)]
    at_c = [c, 1 - c]
    at_z = [(z + d) % 4 for d in range(4)]

    def dev(dx=0, dy=0, dc=0, dz=0):
        return (at_x[dx] + at_y[dy] + at_c[dc], at_z[dz])

    def send(src, dst, ss, rs, target):
        pltpu.make_async_remote_copy(
            src_ref=src, dst_ref=dst, send_sem=ss, recv_sem=rs, device_id=target, device_id_type=MESH
        ).start()

    def wait_all(ref, sem):
        pltpu.make_async_copy(ref, ref, sem).wait()

    def g_copy(k):
        l = STARTS[k] // UT
        part = pl.ds(STARTS[k] % UT * UR, SIZES[k] * UR)
        return pltpu.make_async_copy(
            grads.at[l, :, :, :, part, :], graw.at[l, :, :, :, part, :], g_sem.at[k]
        )

    for k in range(AHEAD):
        g_copy(k).start()
    barrier = pltpu.get_barrier_semaphore()

    near = (dev(dc=1), dev(dx=1), dev(dx=3), dev(dy=1), dev(dy=3), dev(dz=1), dev(dz=3))
    for target in near:
        pl.semaphore_signal(barrier, inc=1, device_id=target, device_id_type=MESH)

    ins = [
        pltpu.make_async_copy(a, b, in_sem.at[i])
        for i, (a, b) in enumerate(
            (
                (params, v_params), (moments, v_moms), (row_stat, v_row), (col_stat, v_col), (hidden, v_hid),
                (cell, v_cell), (input_w, v_iw), (recur_w, v_rw), (gate_bias, v_gb), (head_w, headt),
                (head_bias, v_hb), (w1, v_w1), (w2, v_w2),
            )
        )
    ]
    def load_more(k):
        if k + AHEAD < NC:
            g_copy(k + AHEAD).start()
        if k == 1:
            for copy in ins:
                copy.start()

    def units(k):
        return pl.ds(STARTS[k], SIZES[k])

    def spread(k, core, write):
        l = STARTS[k] // UT

        def step(i, carry):
            a, b = i // 4, i % 4
            for u in range(STARTS[k], STARTS[k] + SIZES[k]):
                v = graw[l, a, b, core, pl.ds(u % UT * UR, UR), :].astype(F32)
                for q in range(4):
                    write(u, q, a if q < 2 else b, b if q < 2 else a, v[q * RQ:(q + 1) * RQ, :])
            return carry

        lax.fori_loop(0, 16, step, 0)

    def stage_d(k):
        g_copy(k).wait()
        load_more(k)

        def write(u, q, i, j, v):
            stage[u, q, i, j] = v

        spread(k, 1 - c, write)
        if k == 0:
            pl.semaphore_wait(barrier, 7)
        send(stage.at[units(k)], acc.at[units(k)], s_sem.at[0], d_rs.at[k], dev(dc=1))

    first = (x, y)
    second = (y, x)
    ways = ((dev(dx=1), dev(dx=3)), (dev(dy=1), dev(dy=3)))
    across = (dev(dx=2), dev(dy=2))

    def stage_1(k):
        wait_all(acc.at[units(k)], d_rs.at[k])

        def write(u, q, i, j, v):
            acc[u, q, i, j] += v

        spread(k, c, write)
        un = units(k)
        if k >= DIRECT_1:
            for h in range(2):
                i0, (plus, minus), both = first[h], ways[h], pl.ds(2 * h, 2)
                send(acc.at[un, both, (i0 + 2) % 4], r1a.at[un, both], s_sem.at[1], r1a_rs.at[k], across[h])
                send(acc.at[un, both, (i0 + 1) % 4], r1b.at[un, both, 0], s_sem.at[2], r1b_rs.at[k], plus)
                send(acc.at[un, both, (i0 + 3) % 4], r1b.at[un, both, 1], s_sem.at[2], r1b_rs.at[k], minus)
            return
        for h in range(2):
            i0, (plus, minus), qa, qb = first[h], ways[h], 2 * h, 2 * h + 1
            send(acc.at[un, qa, (i0 + 2) % 4], r1a.at[un, qa], s_sem.at[1], r1a_rs.at[k], plus)
            send(acc.at[un, qb, (i0 + 2) % 4], r1a.at[un, qb], s_sem.at[1], r1a_rs.at[k], minus)
        for h in range(2):
            i0, (plus, minus), qa, qb = first[h], ways[h], 2 * h, 2 * h + 1
            send(acc.at[un, qb, (i0 + 1) % 4], r1b.at[un, qb, 0], s_sem.at[2], r1b_rs.at[k], plus)
            send(acc.at[un, qa, (i0 + 3) % 4], r1b.at[un, qa, 1], s_sem.at[2], r1b_rs.at[k], minus)

    def stage_2(k):
        if k >= DIRECT_1:
            return
        un = units(k)
        wait_all(r1a.at[un], r1a_rs.at[k])
        for h in range(2):
            i0, (plus, minus), qa, qb = first[h], ways[h], 2 * h, 2 * h + 1
            acc[un, qa, (i0 + 1) % 4] += r1a[un, qa]
            send(acc.at[un, qa, (i0 + 1) % 4], r1b.at[un, qa, 0], s_sem.at[2], r1b_rs.at[k], plus)
            acc[un, qb, (i0 + 3) % 4] += r1a[un, qb]
            send(acc.at[un, qb, (i0 + 3) % 4], r1b.at[un, qb, 1], s_sem.at[2], r1b_rs.at[k], minus)

    def stage_3(k):
        un = units(k)
        wait_all(r1b.at[un], r1b_rs.at[k])
        if k >= DIRECT_1:
            wait_all(r1a.at[un], r1a_rs.at[k])
        for h in range(2):
            i0, j0, (plus, minus), qa, qb = first[h], second[h], ways[1 - h], 2 * h, 2 * h + 1
            for q in (qa, qb):
                got = r1b[un, q, 0] + r1b[un, q, 1]
                if k >= DIRECT_1:
                    got = got + r1a[un, q]
                acc[un, q, i0] += got
            if k >= DIRECT_2:
                both = pl.ds(2 * h, 2)
                send(acc.at[un, both, i0, (j0 + 2) % 4], r2a.at[un, both], s_sem.at[3], r2a_rs.at[k], across[1 - h])
                send(acc.at[un, both, i0, (j0 + 1) % 4], r2b.at[un, both, 0], s_sem.at[4], r2b_rs.at[k], plus)
                send(acc.at[un, both, i0, (j0 + 3) % 4], r2b.at[un, both, 1], s_sem.at[4], r2b_rs.at[k], minus)
                continue
            send(acc.at[un, qa, i0, (j0 + 2) % 4], r2a.at[un, qa], s_sem.at[3], r2a_rs.at[k], plus)
            send(acc.at[un, qb, i0, (j0 + 2) % 4], r2a.at[un, qb], s_sem.at[3], r2a_rs.at[k], minus)
            send(acc.at[un, qb, i0, (j0 + 1) % 4], r2b.at[un, qb, 0], s_sem.at[4], r2b_rs.at[k], plus)
            send(acc.at[un, qa, i0, (j0 + 3) % 4], r2b.at[un, qa, 1], s_sem.at[4], r2b_rs.at[k], minus)

    def stage_4(k):
        if k >= DIRECT_2:
            return
        un = units(k)
        wait_all(r2a.at[un], r2a_rs.at[k])
        for h in range(2):
            i0, j0, (plus, minus), qa, qb = first[h], second[h], ways[1 - h], 2 * h, 2 * h + 1
            acc[un, qa, i0, (j0 + 1) % 4] += r2a[un, qa]
            send(acc.at[un, qa, i0, (j0 + 1) % 4], r2b.at[un, qa, 0], s_sem.at[4], r2b_rs.at[k], plus)
            acc[un, qb, i0, (j0 + 3) % 4] += r2a[un, qb]
            send(acc.at[un, qb, i0, (j0 + 3) % 4], r2b.at[un, qb, 1], s_sem.at[4], r2b_rs.at[k], minus)

    def stage_5(k):
        l = STARTS[k] // UT
        wait_all(r2b.at[units(k)], r2b_rs.at[k])
        if k >= DIRECT_2:
            wait_all(r2a.at[units(k)], r2a_rs.at[k])
        for u in range(STARTS[k], STARTS[k] + SIZES[k]):
            for q in range(4):
                span = pl.ds(u % UT * UR + q * RQ, RQ)
                g = acc[u, q, first[q // 2], second[q // 2]] + r2b[u, q, 0] + r2b[u, q, 1]
                if k >= DIRECT_2:
                    g = g + r2a[u, q]
                gsum[l, span, :] = g
                sq = g * g
                rowrep[l, span, :] = jnp.broadcast_to(jnp.sum(sq, 1, keepdims=True), (RQ, 128))
                colacc[l] += sq
                for n in range(3):
                    m = DECAYS[n] * v_moms[n, l, span, :] + (np.float32(1) - DECAYS[n]) * g
                    n_moms[n, l, span, :] = m
                    macc[l, n] += m * m

    lane = lax.broadcasted_iota(jnp.int32, (1, 128), 1)

    def prepare_0():
        for copy in ins:
            copy.wait()
        colacc[...] = jnp.zeros_like(colacc)
        macc[...] = jnp.zeros_like(macc)
        for l in range(L):
            def square(i, s):
                v = v_params[l, pl.ds(pl.multiple_of(i * 8, 8), 8), :]
                return s + v * v

            squares = lax.fori_loop(0, RB // 8, square, jnp.zeros((8, CB), F32))
            zero = jnp.zeros((1, 1), F32)
            early[l] = put([zero] * 4 + [total(squares), jnp.sum(v_row[l:l + 1, :], 1, keepdims=True)])
        recsum[...] = jnp.zeros_like(recsum)
        reps = [jnp.concatenate([lane_to_rows(v_hid[l:l + 1, i * 128:(i + 1) * 128]) for i in range(4)], 0) for l in range(L)]
        for l in range(L):
            hidrep[l] = reps[l]

    def recurrent(begin, end):
        def recur(i, sums):
            at = pl.ds(pl.multiple_of(i * 8, 8), 8)
            w = v_rw[at, :]
            return tuple(sums[l] + w * jnp.tile(hidrep[l, at, :], (1, 16)) for l in range(L))

        sums = lax.fori_loop(begin, end, recur, tuple(recsum[l] for l in range(L)))
        for l in range(L):
            recsum[l] = sums[l]

    def prepare_1():
        recurrent(0, H // 16)

    def prepare_2():
        recurrent(H // 16, H // 8)
        for l in range(L):
            pre[l] = jnp.sum(recsum[l], 0, keepdims=True) + v_gb[...]

    def prepare_3():
        hbcol[...] = lane_to_rows(jnp.concatenate([v_hb[...], jnp.zeros((1, 126 - HID), F32)], 1))[0:HID + 2, :]
        w1t = jnp.concatenate([v_w1[...], jnp.zeros((128 - NF, HID), F32)], 0)
        w1t = jnp.transpose(jnp.concatenate([w1t, jnp.zeros((128, 128 - HID), F32)], 1))[0:HID, :]
        at = lax.broadcasted_iota(jnp.int32, (HID, 256), 1)
        wide = jnp.zeros((HID, 256), F32)
        for n in range(NF):
            hit = ((at // 8) % NF == n) & (at < 144)
            wide = jnp.where(hit, jnp.broadcast_to(w1t[:, n:n + 1], (HID, 256)), wide)
        tall = jnp.broadcast_to(wide[:, None, :], (HID, 8, 256)).reshape(HID * 8, 256)
        tall_at = lax.broadcasted_iota(jnp.int32, (HID * 8, 256), 1)
        tall_row = lax.broadcasted_iota(jnp.int32, (HID * 8, 256), 0)
        tall = jnp.where(tall_at % 8 == tall_row % 8, tall, 0.0)
        high = tall.astype(BF16).astype(F32)
        tall = jnp.where(tall_at < 96, high, tall - high).astype(BF16)
        for l in range(L):
            wst[l] = tall
        for o in range(2):
            row = jnp.concatenate([v_w2[o:o + 1, :], jnp.zeros((1, 128 - HID), F32)], 1)
            w2rep[o] = lane_to_rows(row)[0:HID, :]

    def total(v):
        return jnp.sum(jnp.sum(v, 0, keepdims=True), 1, keepdims=True)

    def put(values):
        row = jnp.zeros((1, 128), F32)
        for j, v in enumerate(values):
            row = jnp.where(lane == j, v, row)
        return row

    def pick(row, j):
        return jnp.sum(jnp.where(lane == j, row, 0.0), 1, keepdims=True)

    def exchange(l):
        sums = [colacc[l], macc[l, 0], macc[l, 1], macc[l, 2]]
        pa[l, :, 0:128] = early[l] + put([total(v) for v in sums])
        pa[l, :, 128:384] = jnp.sum(colacc[l], 0, keepdims=True)
        send(pa.at[l], cr.at[l], c_ss.at[l], c_rs.at[l], dev(dc=1))
        for i in range(2):
            zb[l, :, (i + 1) * 128:(i + 2) * 128] = rows_to_lane(rowrep[l, i * 128:(i + 1) * 128, :])

    def announce(l):
        wait_all(cr.at[l], c_rs.at[l])
        pb[l] = pa[l] + cr[l]
        zb[l, :, 0:128] = pb[l, :, 0:128]

        def others(n, dz):
            for j in range(1, 16):
                send(
                    pb.at[l, :, pl.ds(0, 128)], sr.at[l, 15 * n + j - 1], o_ss.at[l], o_rs.at[l], dev(j // 4, j % 4, 0, dz)
                )

        others(0, 2)
        for j in range(1, 16):
            send(pb.at[l], pr.at[l, j - 1], p_ss.at[l], p_rs.at[l], dev(j // 4, j % 4))
        others(1, 3)
        others(2, 1)
        for dz in range(1, 4):
            send(zb.at[l], zr.at[l, dz - 1], z_ss.at[l], z_rs.at[l], dev(dz=dz))

    def control(l):
        wait_all(zr.at[l], z_rs.at[l])
        got = zb[l] + zr[l, 0] + zr[l, 1] + zr[l, 2]
        new = 0.9 * v_row[l:l + 1, :] + 0.1 * got[:, 128:384] / KV
        n_rows[l:l + 1, :] = new
        for i in range(2):
            rowrep[l, i * 128:(i + 1) * 128, :] = lane_to_rows(new[:, i * 128:(i + 1) * 128])
        wait_all(pr.at[l], p_rs.at[l])
        near = jnp.sum(pr[l], 0)
        new = 0.9 * v_col[l:l + 1, :] + 0.1 * (pb[l, :, 128:384] + near[:, 128:384]) / D
        n_cols[l:l + 1, :] = new
        wait_all(sr.at[l], o_rs.at[l])
        sums = got[:, 0:128] + near[:, 0:128] + jnp.sum(sr[l], 0)
        means = sums / (D * KV)
        stats = jnp.log(means + 1e-06)
        gates = pre[l]
        for j in range(5):
            gates = gates + pick(stats, j) * v_iw[j:j + 1, :]
        i_g = jax.nn.sigmoid(gates[:, 0:H])
        f_g = jax.nn.sigmoid(gates[:, H:2 * H])
        c_g = jnp.tanh(gates[:, 2 * H:3 * H])
        o_g = jax.nn.sigmoid(gates[:, 3 * H:])
        new_cell = f_g * v_cell[l:l + 1, :] + i_g * c_g
        new_hid = o_g * jnp.tanh(new_cell)
        n_cell[l:l + 1, :] = new_cell
        n_hid[l:l + 1, :] = new_hid
        m = jnp.sum(headt[...] * new_hid, 1, keepdims=True) + hbcol[...]
        mod[l, 0:HID + 2, :] = jnp.broadcast_to(m, (HID + 2, 128))
        mod[l, HID:HID + 1, :] = jnp.broadcast_to(jnp.exp(m[HID:HID + 1, :]), (1, 128))
        mod[l, HID + 1:HID + 2, :] = jnp.broadcast_to(0.5 * m[HID + 1:HID + 2, :], (1, 128))
        bias = jnp.broadcast_to(m[0:HID, None, :], (HID, 8, 128)).reshape(HID * 8, 128)
        high = bias.astype(BF16).astype(F32)
        side = wst[l, :, 128:256].astype(F32)
        side = jnp.where(lane == 16, high, jnp.where(lane == 17, bias - high, side))
        wst[l, :, 128:256] = side.astype(BF16)
        row_mean = (0.9 * (pick(sums, 5) / 4) + 0.1 * pick(sums, 0) / KV) / D
        colrow[l] = new / row_mean
        norms[l, 0:1, :] = jnp.broadcast_to(lax.rsqrt(pick(means, 4) + 1e-06), (1, 128))
        norms[l, 1:2, :] = jnp.broadcast_to(lax.rsqrt(pick(means, 0) + 1e-06), (1, 128))

    def network_0(begin, end):
        network(
            begin, end, gsum.at[0], [n_moms.at[n, 0] for n in range(3)], v_params.at[0], rowrep.at[0], colrow.at[0],
            norms.at[0], wst.at[0], w2rep, mod.at[0], n_params,
        )

    def meet(n):
        for target in (dev(dz=1), dev(dz=3)):
            pl.semaphore_signal(met.at[n], inc=1, device_id=target, device_id_type=MESH)

    steps = (stage_d, stage_1, stage_2, stage_3, stage_4, stage_5)
    for step, k in ORDER:
        if step == "p":
            (prepare_0, prepare_1, prepare_2, prepare_3)[k]()
        elif step == "x":
            exchange(0)
        elif step == "a":
            pl.semaphore_wait(met.at[1], 2)
            announce(0)
        elif step == "c":
            control(0)
        else:
            steps[step](k)
        if step == 5 and k == 0:
            meet(0)
        if step == 5 and k == 1:
            pl.semaphore_wait(met.at[0], 2)
            meet(1)
    exchange(1)
    announce(1)
    network_0(0, 4)
    wait_all(acc, s_sem.at[0])
    wait_all(r1a, s_sem.at[1])
    wait_all(r1b, s_sem.at[2])
    wait_all(r2a, s_sem.at[3])
    wait_all(r2b, s_sem.at[4])
    control(1)
    for l in range(L):
        wait_all(cr.at[l], c_ss.at[l])
        wait_all(zr.at[l], z_ss.at[l])
        wait_all(pr.at[l], p_ss.at[l])
        wait_all(sr.at[l], o_ss.at[l])


def finish(
    params_0, moms, params, gsum, rowrep, colrow, norms, wst, w2rep, mod, rows, cols, hid, cell,
    o_params, o_moms, o_rows, o_cols, o_hid, o_cell, params_1, sem,
):
    copies = [
        pltpu.make_async_copy(a, b, sem.at[i])
        for i, (a, b) in enumerate(
            ((moms, o_moms), (params_0, o_params.at[0]), (rows, o_rows), (cols, o_cols), (hid, o_hid), (cell, o_cell))
        )
    ]
    for copy in copies:
        copy.start()
    for part in range(2):
        network(
            2 * part, 2 * part + 2, gsum.at[1], [moms.at[n, 1] for n in range(3)], params.at[1], rowrep.at[1],
            colrow.at[1], norms.at[1], wst.at[1], w2rep, mod.at[1], params_1,
        )
        half = pl.ds(part * RB // 2, RB // 2)
        copy = pltpu.make_async_copy(params_1.at[half, :], o_params.at[1, half, :], sem.at[6 + part])
        copy.start()
        copies.append(copy)
    for copy in copies:
        copy.wait()


def body(grads, params, moments, row_stat, col_stat, hidden, cell, input_w, recur_w, gate_bias, head_w, head_bias, w1, w2):
    hbm = pl.BlockSpec(memory_space=pltpu.HBM)
    held = pl.BlockSpec(memory_space=pltpu.VMEM)
    vmem = pltpu.VMEM
    dma = pltpu.SemaphoreType.DMA
    quarter = (RQ, CB)
    between = (
        vmem((RB, CB), F32),
        vmem((3, L, RB, CB), F32),
        vmem((L, RB, CB), F32),
        vmem((L, RB, CB), F32),
        vmem((L, RB, 128), F32),
        vmem((L, 1, CB), F32),
        vmem((L, 2, 128), F32),
        vmem((L, HID * 8, 256), BF16),
        vmem((2, HID, 128), F32),
        vmem((L, HID + 2, 128), F32),
        vmem((L, RB), F32),
        vmem((L, CB), F32),
        vmem((L, H), F32),
        vmem((L, H), F32),
    )
    operands = (
        grads.reshape(L, 4, 4, 2, RB, CB), params, moments, row_stat, col_stat, hidden, cell, input_w, recur_w,
        gate_bias.reshape(1, 4 * H), head_w.T, head_bias.reshape(1, HID + 2), w1, w2.T,
    )
    results = pl.pallas_call(
        kernel,
        out_shape=between,
        in_specs=[hbm] * 14,
        out_specs=(held,) * len(between),
        scratch_shapes=[
            vmem((L, 4, 4, 2, RB, CB), BF16),
            vmem((NU, 4, 4, 4) + quarter, F32),
            vmem((NU, 4, 4, 4) + quarter, F32),
            vmem((NU, 4, 4) + quarter, F32),
            vmem((NU, 4, 2, 4) + quarter, F32),
            vmem((NU, 4) + quarter, F32),
            vmem((NU, 4, 2) + quarter, F32),
            vmem((3, L, RB, CB), F32),
            vmem((L, RB), F32),
            vmem((L, CB), F32),
            vmem((L, H), F32),
            vmem((L, H), F32),
            vmem((5, 4 * H), F32),
            vmem((H, 4 * H), F32),
            vmem((1, 4 * H), F32),
            vmem((HID + 2, H), F32),
            vmem((1, HID + 2), F32),
            vmem((NF, HID), F32),
            vmem((2, HID), F32),
            vmem((L, H, 128), F32),
            vmem((L, 8, 4 * H), F32),
            vmem((L, 8, CB), F32),
            vmem((L, 3, 8, CB), F32),
            vmem((L, 1, 128), F32),
            vmem((L, 1, 4 * H), F32),
            vmem((HID + 2, 128), F32),
            vmem((L, 1, 384), F32),
            vmem((L, 1, 384), F32),
            vmem((L, 1, 384), F32),
            vmem((L, 1, 384), F32),
            vmem((L, 3, 1, 384), F32),
            vmem((L, 15, 1, 384), F32),
            vmem((L, 45, 1, 128), F32),
            dma((13,)),
            dma((NC,)),
            dma((5,)),
        ]
        + [dma((NC,))] * 5
        + [dma((L,))] * 8
        + [pltpu.SemaphoreType.REGULAR((2,))],
        compiler_params=pltpu.CompilerParams(
            collective_id=0, has_side_effects=True, vmem_limit_bytes=46 * 2**20
        ),
        name="update",
    )(*[pltpu.with_memory_space_constraint(v, pltpu.HBM) for v in operands])
    return pl.pallas_call(
        finish,
        out_shape=(
            jax.ShapeDtypeStruct((L, RB, CB), F32),
            jax.ShapeDtypeStruct((3, L, RB, CB), F32),
            jax.ShapeDtypeStruct((L, RB), F32),
            jax.ShapeDtypeStruct((L, CB), F32),
            jax.ShapeDtypeStruct((L, H), F32),
            jax.ShapeDtypeStruct((L, H), F32),
        ),
        in_specs=[held] * len(between),
        out_specs=(hbm,) * 6,
        scratch_shapes=[vmem((RB, CB), F32), dma((8,))],
        compiler_params=pltpu.CompilerParams(vmem_limit_bytes=16 * 2**20),
        name="finish",
    )(*results)


def solution(mesh):
    return jax.shard_map(
        body,
        mesh=mesh,
        in_specs=(
            P("dp", None, None, "tensor"),
            P(None, "dp", "tensor"),
            P(None, None, "dp", "tensor"),
            P(None, "dp"),
            P(None, "tensor"),
        )
        + (P(),) * 9,
        out_specs=(
            P(None, "dp", "tensor"),
            P(None, None, "dp", "tensor"),
            P(None, "dp"),
            P(None, "tensor"),
            P(),
            P(),
        ),
        check_vma=False,
    )
```
